256 devices in a mesh: ctx: 64 (over y_lo, x, z), tp: 4 (over y_hi, core).
Axes of the slice: x: 4, y: 4 (y_hi: 2, y_lo: 2; y = y_hi * 2 + y_lo), z: 8, core: 2. Of those that a mesh axis runs over, the one named last changes fastest.
Arguments:
- q_pre: bfloat16 [2, 4096, 4096], P(None, 'ctx', 'tp'), may hold values from -8 to 8
- k_pre: bfloat16 [2, 4096, 512], P(None, 'ctx', 'tp'), may hold values from -8 to 8
- value_before_filter: bfloat16 [2, 4096, 512], P(None, 'ctx', 'tp'), may hold values from -8 to 8
- d_out: bfloat16 [2, 4096, 4096], P(None, 'ctx', 'tp'), may hold values from -8 to 8
- filters: float32 [3, 3, 128], replicated, may hold values from 0.5 to 1.5
- doc_lengths: int32 [8], replicated, may hold values from 1 to 4096, 8192 in all
Outputs:
- d_q_pre: float32 [2, 4096, 4096], P(None, 'ctx', 'tp')
- d_k_pre: float32 [2, 4096, 512], P(None, 'ctx', 'tp')
- d_v_pre: float32 [2, 4096, 512], P(None, 'ctx', 'tp')
- d_filters: float32 [3, 3, 128], replicated
The draws below stay inside these ranges and needn't reach their ends.
Inputs may be any that keep to these rules, and one draw needn't show every extreme that they name: `doc_lengths`: the lengths sum to 8192, and the longest document has exactly 4096 positions.
All inputs are finite; a program needn't handle non-finite values.
Results may differ from the reference program's by a relative error of at most 0.009.
The reference program's roundings to bfloat16 on the way count: a program that leaves them out, or rounds other values in their place, can miss the bound.
Values may be sent and summed in bfloat16 or wider, within the bound.
A program may use at most 128 MiB of HBM per device.

```python
import math
import jax
import jax.numpy as jnp
import numpy as np
from jax import lax

HEAD_WIDTH = 128
HQ = 32
KEY_VALUE_HEADS = 4
QUERY_GROUP = 8
SPAN = 64
HALF_LENGTH = 4096
PACKED_LENGTH = 8192
DOCS = 8
TAPS = 3
N_CTX = 64


def draw_q_pre(key, part):
    key = jax.random.fold_in(key, 3)
    sampled_values = jnp.clip(jax.random.normal(key, (2, HALF_LENGTH, HQ * HEAD_WIDTH)), -8.0, 8.0)
    return sampled_values.astype(jnp.bfloat16)


def draw_k_pre(key, part):
    key = jax.random.fold_in(key, 5)
    sampled_values = jnp.clip(jax.random.normal(key, (2, HALF_LENGTH, KEY_VALUE_HEADS * HEAD_WIDTH)), -8.0, 8.0)
    return sampled_values.astype(jnp.bfloat16)


def levels(rng, extent, cuts, smallest, largest):
    gain, own = 1.0, jax.random.fold_in(rng, 6)
    for axis_at, parts in cuts:
        steps = jnp.exp(jax.random.uniform(jax.random.fold_in(own, axis_at), (parts,), jnp.float32, smallest / len(cuts), largest / len(cuts)))
        gain = gain * jnp.repeat(steps, extent[axis_at] // parts).reshape([-1 if axis == axis_at else 1 for axis in range(len(extent))])
    return gain


def split_up(number_of, total, bound, lean):
    loads = [(1 << 20) // math.isqrt(rank ** lean) + 1 for rank in range(2, number_of + 1)]
    spare, given = total - bound - (number_of - 1), [1] * (number_of - 1)
    while spare > 0:
        candidates = [i for i in range(number_of - 1) if given[i] < bound]
        pool, remaining = sum([loads[i] for i in candidates]), spare
        for i in candidates:
            more = min(bound - given[i], max(1, remaining * loads[i] // pool), spare)
            given[i] = given[i] + more
            spare = spare - more
    return np.array([bound] + given)


def uneven_parts(stream_key, amount, total, limit, skew):
    if amount == 2:
        one = jax.random.randint(stream_key, (), max(1, total - limit), min(limit, total - 1) + 1)
        return jnp.stack([one, total - one])
    tallies = jnp.asarray(split_up(amount, total, limit, skew), jnp.int32)
    twos = (amount - 1) // 2
    giver, taker = tallies[1:1 + 2 * twos:2], tallies[2:2 + 2 * twos:2]
    room = jnp.minimum(giver - 1, limit - taker)
    passed = jax.random.randint(jax.random.fold_in(stream_key, 1), (twos,), 0, 1 << 20) % (room + 1)
    tallies = tallies.at[1:1 + 2 * twos:2].set(giver - passed).at[2:2 + 2 * twos:2].set(taker + passed)
    return tallies[jax.random.permutation(jax.random.fold_in(stream_key, 2), amount)]


def noise(key, extent, width, most, cuts=(), kind=jnp.bfloat16):
    factor_of = levels(key, extent, cuts, -0.22, 0.18) if cuts else 1.0
    array = jax.random.normal(key, extent, jnp.float32) * width * factor_of
    return jnp.minimum(jnp.maximum(array, -most), most).astype(kind)


def setup_inputs(seed: int = 0) -> dict:
    arg_keys = jax.random.split(jax.random.key(seed), 7)
    return {
        "q_pre": draw_q_pre(jax.random.fold_in(arg_keys[6], 71), 0),
        "k_pre": draw_k_pre(jax.random.fold_in(arg_keys[6], 71), 0),
        "value_before_filter": noise(arg_keys[2], (2, HALF_LENGTH, KEY_VALUE_HEADS * HEAD_WIDTH), 1.0, 8.0, ((1, 64), (2, 4))),
        "d_out": noise(arg_keys[3], (2, HALF_LENGTH, HQ * HEAD_WIDTH), 1.0, 8.0, ((1, 64), (2, 4))),
        "filters": jnp.clip(jax.random.uniform(arg_keys[4], (3, TAPS, HEAD_WIDTH), jnp.float32, 0.5, 1.5), 0.5, 1.5),
        "doc_lengths": uneven_parts(arg_keys[5], DOCS, PACKED_LENGTH, PACKED_LENGTH // 2, 2).astype(jnp.int32),
    }


def to_sequence(layout):
    late_rows = layout[1].reshape(N_CTX, SPAN, -1)[::-1].reshape(HALF_LENGTH, -1)
    return jnp.concatenate([layout[0], late_rows], axis=0)

def to_layout(sequence):
    late_rows = sequence[HALF_LENGTH:].reshape(N_CTX, SPAN, -1)[::-1].reshape(HALF_LENGTH, -1)
    return jnp.stack([sequence[:HALF_LENGTH], late_rows])

def doc_index(places, starts):
    return lax.optimization_barrier(jnp.sum((places[..., None] >= starts).astype(jnp.int32), axis=-1)) - 1

def convolve(source, weights, doc_ids):
    head_count = source.shape[1] // HEAD_WIDTH
    grid_rows = source.reshape(PACKED_LENGTH, head_count, HEAD_WIDTH)
    summed = jnp.zeros((PACKED_LENGTH, head_count, HEAD_WIDTH), jnp.float32)
    for tap_index in range(TAPS):
        earlier = jnp.concatenate([jnp.zeros((tap_index, head_count, HEAD_WIDTH), source.dtype), grid_rows[:PACKED_LENGTH - tap_index]], axis=0)
        earlier_docs = jnp.concatenate([jnp.full((tap_index,), -1, jnp.int32), doc_ids[:PACKED_LENGTH - tap_index]])
        same_doc = earlier_docs == doc_ids
        summed = summed + jnp.where(same_doc[:, None, None], weights[tap_index] * earlier, 0.0)
    return summed.reshape(PACKED_LENGTH, head_count * HEAD_WIDTH)

def attention_grads(query_full, key_full, value_full, output_gradient, doc_ids):
    query_head_rows = jnp.transpose(query_full.reshape(PACKED_LENGTH, KEY_VALUE_HEADS, QUERY_GROUP, HEAD_WIDTH), (1, 0, 2, 3))
    gradient_per_head = jnp.transpose(output_gradient.reshape(PACKED_LENGTH, KEY_VALUE_HEADS, QUERY_GROUP, HEAD_WIDTH), (1, 0, 2, 3))
    key_head_rows = jnp.transpose(key_full.reshape(PACKED_LENGTH, KEY_VALUE_HEADS, HEAD_WIDTH), (1, 0, 2))
    value_head_rows = jnp.transpose(value_full.reshape(PACKED_LENGTH, KEY_VALUE_HEADS, HEAD_WIDTH), (1, 0, 2))
    places = jnp.arange(PACKED_LENGTH, dtype=jnp.int32)
    block_size = math.gcd(PACKED_LENGTH, 512)
    score_scale = HEAD_WIDTH ** (-0.5)

    def per_head(operands):
        q_head, k_head, v_head, grad_head = operands
        dq_blocks = []
        dk_total = jnp.zeros((PACKED_LENGTH, HEAD_WIDTH), jnp.float32)
        dv_total = jnp.zeros((PACKED_LENGTH, HEAD_WIDTH), jnp.float32)
        for block_index in range(PACKED_LENGTH // block_size):
            row_lower = block_index * block_size
            row_upper = row_lower + block_size
            queries = q_head[row_lower:row_upper].astype(jnp.float32)
            grads_out = grad_head[row_lower:row_upper].astype(jnp.float32)
            key_rows = k_head[:row_upper].astype(jnp.float32)
            value_rows = v_head[:row_upper].astype(jnp.float32)
            allowed = (doc_ids[row_lower:row_upper, None] == doc_ids[None, :row_upper]) & (places[None, :row_upper] <= places[row_lower:row_upper, None])
            scores = jnp.einsum('cgd,nd->gcn', queries, key_rows) * score_scale
            row_max = lax.optimization_barrier(jnp.max(jnp.where(allowed, scores, -jnp.inf), axis=-1, keepdims=True))
            exp_total = lax.optimization_barrier(jnp.sum(jnp.where(allowed, jnp.exp(scores - row_max), 0.0), axis=-1, keepdims=True))
            log_total = row_max + jnp.log(exp_total)
            probabilities = jnp.where(allowed, jnp.exp(scores - log_total), 0.0)
            prob_grads = jnp.einsum('cgd,nd->gcn', grads_out, value_rows)
            row_sums = lax.optimization_barrier(jnp.sum(probabilities * prob_grads, axis=-1, keepdims=True))
            probs_low = lax.optimization_barrier(probabilities.astype(jnp.bfloat16)).astype(jnp.float32)
            score_grads = probabilities * (prob_grads - row_sums) * score_scale
            grads_low = lax.optimization_barrier(score_grads.astype(jnp.bfloat16)).astype(jnp.float32)
            dv_total = dv_total.at[:row_upper].add(jnp.einsum('gcn,cgd->nd', probs_low, grads_out))
            dk_total = dk_total.at[:row_upper].add(jnp.einsum('gcn,cgd->nd', grads_low, queries))
            dq_blocks.append(jnp.einsum('gcn,nd->cgd', grads_low, key_rows))
        return (jnp.concatenate(dq_blocks, axis=0), dk_total, dv_total)
    dq_heads, key_gradient_heads, value_gradient_heads = lax.map(per_head, (query_head_rows, key_head_rows, value_head_rows, gradient_per_head))
    dq_all = jnp.transpose(dq_heads, (1, 0, 2, 3)).reshape(PACKED_LENGTH, HQ * HEAD_WIDTH)
    key_gradient_full = jnp.transpose(key_gradient_heads, (1, 0, 2)).reshape(PACKED_LENGTH, KEY_VALUE_HEADS * HEAD_WIDTH)
    value_gradient_full = jnp.transpose(value_gradient_heads, (1, 0, 2)).reshape(PACKED_LENGTH, KEY_VALUE_HEADS * HEAD_WIDTH)
    return (dq_all, key_gradient_full, value_gradient_full)

def reference(q_pre, k_pre, value_before_filter, d_out, filters, doc_lengths):
    starts = jnp.cumsum(doc_lengths) - doc_lengths
    doc_ids = doc_index(jnp.arange(PACKED_LENGTH, dtype=jnp.int32), starts)
    sources = [to_sequence(array_in).astype(jnp.float32) for array_in in (q_pre, k_pre, value_before_filter)]
    projected = []
    pullbacks = []
    for tensor_index in range(3):
        conv_out, pullback = jax.vjp(lambda data, weights: convolve(data, weights, doc_ids), sources[tensor_index], filters[tensor_index])
        projected.append(conv_out.astype(jnp.bfloat16))
        pullbacks.append(pullback)
    grads_all = attention_grads(projected[0], projected[1], projected[2], to_sequence(d_out), doc_ids)
    results = [pullbacks[tensor_index](grads_all[tensor_index]) for tensor_index in range(3)]
    d_filters = jnp.stack([results[tensor_index][1] for tensor_index in range(3)])
    return (to_layout(results[0][0]), to_layout(results[1][0]), to_layout(results[2][0]), d_filters)
```

```python
import functools
import math

import jax
import jax.numpy as jnp
from jax import lax
from jax.experimental import pallas as pl
from jax.experimental.pallas import tpu as pltpu
from jax.sharding import PartitionSpec as P

MESH = pl.DeviceIdType.MESH
Y, X, Z = 0, 1, 2
SIZES = (2, 4, 8)
CTX = 64
TP = 4
ROWS = 64
LENGTH = 8192
HEADS = 8
WIDTH = 128
COLS = HEADS * ROWS
TILE = 256
N_TILES = LENGTH // TILE
MAX_TILES = 18
SCALE = WIDTH ** (-0.5)
LOG2E = math.log2(math.e)
F32 = jnp.float32
BF16 = jnp.bfloat16

PLAN = (
    (0, 0, 0, 32, (Y, X, Z)),
    (1, 0, 0, 32, (Y, Z, X)),
    (0, 1, 0, 32, (Z, X, Y)),
    (1, 1, 0, 32, (Y, Z, X)),
    (0, 0, 32, 32, (Y, X, Z)),
    (1, 0, 32, 32, (X, Z, Y)),
    (0, 1, 32, 32, (Y, Z, X)),
    (1, 1, 32, 32, (Z, X, Y)),
)
SLOTS = 13


def gather_hops(n):
    if n == 2:
        return [[(1, 0, None)]]
    if n == 4:
        return [[(1, 0, None), (-1, 0, None)], [(1, -1, 0), (-1, 1, 1)]]
    return [
        [(1, 0, None), (-1, 0, None)],
        [(1, -1, None), (-1, 1, None)],
        [(1, -2, None), (-1, 2, None)],
        [(1, -3, 0), (-1, 3, 1)],
    ]


def coords():
    c = lax.axis_index("ctx")
    return [c // 32, (c // 8) % 4, c % 8]


def ctx_of(co):
    return co[0] * 32 + co[1] * 8 + co[2]


def shifted(co, dim, by):
    co = list(co)
    co[dim] = (co[dim] + by + SIZES[dim]) % SIZES[dim]
    return co


def block_at(half, dim, at):
    return at if half == 0 else SIZES[dim] - 1 - at


def gather_kernel(k_ref, v_ref, q_ref, g_ref, rim_ref, send_sem, recv_sem, rim_send, rim_recv):
    c = lax.axis_index("ctx")
    co = coords()
    after, before = (c + 1) % CTX, (c + CTX - 1) % CTX
    neighbours = [ctx_of(shifted(co, Y, 1)), after, before]
    for dim in (X, Z):
        neighbours += [ctx_of(shifted(co, dim, 1)), ctx_of(shifted(co, dim, -1))]
    barrier = pltpu.get_barrier_semaphore()
    for neighbour in neighbours:
        pl.semaphore_signal(barrier, inc=1, device_id={"ctx": neighbour}, device_id_type=MESH)
    for half in range(2):
        at = [block_at(half, d, co[d]) for d in range(3)]
        g_ref[0, half, at[0], at[1], at[2]] = k_ref[half]
        g_ref[1, half, at[0], at[1], at[2]] = v_ref[half]
    pl.semaphore_wait(barrier, len(neighbours))

    rims = []
    for half, target in ((0, after), (1, before)):
        copy = pltpu.make_async_remote_copy(
            src_ref=q_ref.at[half, pl.ds(ROWS - 16, 16)],
            dst_ref=rim_ref.at[half],
            send_sem=rim_send.at[half],
            recv_sem=rim_recv.at[half],
            device_id={"ctx": target},
            device_id_type=MESH,
        )
        copy.start()
        rims.append(copy)

    def start(chunk, slot, stage, direction, offset, part):
        which, half, row, rows, order = PLAN[chunk]
        dim = order[stage]
        at = [None] * 3
        for s, d in enumerate(order):
            if s < stage:
                at[d] = pl.ds(0, SIZES[d])
            else:
                at[d] = block_at(half, d, shifted(co, d, offset if s == stage else 0)[d])
        if part is not None:
            rows = rows // 2
            row = row + part * rows
        ref = g_ref.at[which, half, at[0], at[1], at[2], pl.ds(row, rows)]
        copy = pltpu.make_async_remote_copy(
            src_ref=ref,
            dst_ref=ref,
            send_sem=send_sem.at[chunk, slot],
            recv_sem=recv_sem.at[chunk, slot],
            device_id={"ctx": ctx_of(shifted(co, dim, direction))},
            device_id_type=MESH,
        )
        copy.start()
        return copy

    hops = []
    for plan in PLAN:
        steps, slot = [], 0
        for stage, dim in enumerate(plan[4]):
            for at, hop in enumerate(gather_hops(SIZES[dim])):
                steps.append((at == 0, [(slot + i, stage) + entry for i, entry in enumerate(hop)]))
                slot += len(hop)
        hops.append(steps)
    copies, flying = [], [[] for _ in PLAN]
    for hop in range(len(hops[0])):
        for chunk in range(len(PLAN)):
            first, entries = hops[chunk][hop]
            if first:
                for copy in flying[chunk]:
                    copy.wait_recv()
            started = []
            for i, entry in enumerate(entries):
                if not first:
                    flying[chunk][i].wait_recv()
                started.append(start(chunk, *entry))
            flying[chunk] = started
            copies += started
    for chunk in range(len(PLAN)):
        for copy in flying[chunk]:
            copy.wait_recv()
    for copy in rims:
        copy.wait()
    for copy in copies:
        copy.wait_send()


def gather(k, v, q):
    return pl.pallas_call(
        gather_kernel,
        out_shape=(
            jax.ShapeDtypeStruct((2, 2) + SIZES + (ROWS, WIDTH), BF16),
            jax.ShapeDtypeStruct((2, 16, HEADS * WIDTH), BF16),
        ),
        in_specs=[pl.BlockSpec(memory_space=pltpu.VMEM)] * 3,
        out_specs=(pl.BlockSpec(memory_space=pltpu.VMEM),) * 2,
        scratch_shapes=[
            pltpu.SemaphoreType.DMA((len(PLAN), SLOTS)),
            pltpu.SemaphoreType.DMA((len(PLAN), SLOTS)),
            pltpu.SemaphoreType.DMA((2,)),
            pltpu.SemaphoreType.DMA((2,)),
        ],
        compiler_params=pltpu.CompilerParams(
            collective_id=1, has_side_effects=True, vmem_limit_bytes=32 << 20
        ),
        name="gather",
    )(k, v, q)


def doc_starts(lengths_ref):
    starts = [jnp.int32(0)]
    for d in range(7):
        starts.append(starts[-1] + lengths_ref[d])
    return starts


def start_of(places, starts):
    found = jnp.zeros_like(places)
    for s in starts[1:]:
        found = jnp.where(places >= s, s, found)
    return found


def attend_kernel(
    lengths_ref, filters_ref, q_ref, rim_ref, do_ref, g_ref,
    dq_ref, out_ref, taps_ref,
    kc_ref, vc_ref, s_ref, dp_ref, dk_ref, dv_ref, qs_ref, dos_ref, dqt_ref,
):
    c = lax.axis_index("ctx")
    starts = doc_starts(lengths_ref)
    ends = (c * ROWS, (2 * CTX - 1 - c) * ROWS)
    first_tiles, last_tiles = [], []
    for half in range(2):
        first_tiles.append(start_of(ends[half], starts) // TILE)
        last_tiles.append((ends[half] + ROWS + TILE - 1) // TILE)

    def clear(tile, _):
        r0 = pl.multiple_of(tile * TILE, TILE)
        dk_ref[pl.ds(r0, TILE)] = jnp.zeros((TILE, WIDTH), F32)
        dv_ref[pl.ds(r0, TILE)] = jnp.zeros((TILE, WIDTH), F32)
        return 0

    lax.fori_loop(0, N_TILES, clear, 0)

    def q_window(half, h):
        lanes = slice(h * WIDTH, (h + 1) * WIDTH)
        before = rim_ref[half, :, lanes]
        if half == 1:
            before = jnp.where(c == CTX - 1, q_ref[0, ROWS - 16 :, lanes], before)
        cat = jnp.concatenate([before.astype(F32), q_ref[half, :, lanes].astype(F32)], axis=0)
        return [cat[16 - s : 16 - s + ROWS] for s in range(3)]

    def q_masks(half):
        places = ends[half] + lax.broadcasted_iota(jnp.int32, (ROWS, WIDTH), 0)
        begin = start_of(places, starts)
        return [places - s >= begin for s in range(1, 3)]

    for half in range(2):
        masks = q_masks(half)
        for h in range(HEADS):
            x = q_window(half, h)
            y = filters_ref[0, 0:1] * x[0]
            for s in range(1, 3):
                y = y + jnp.where(masks[s - 1], filters_ref[0, s : s + 1] * x[s], 0.0)
            qs_ref[half, h * ROWS : (h + 1) * ROWS] = y.astype(BF16)
            dos_ref[half, h * ROWS : (h + 1) * ROWS] = do_ref[half, :, h * WIDTH : (h + 1) * WIDTH]

    def raw_window(which, r0):
        before = g_ref[which, pl.ds(pl.multiple_of(jnp.maximum(r0 - 16, 0), 16), 16)]
        here = g_ref[which, pl.ds(r0, TILE)]
        cat = jnp.concatenate([before.astype(F32), here.astype(F32)], axis=0)
        return [cat[16 - s : 16 - s + TILE] for s in range(3)]

    def tile_masks(r0):
        places = r0 + lax.broadcasted_iota(jnp.int32, (TILE, WIDTH), 0)
        begin = start_of(places, starts)
        return [places - s >= begin for s in range(1, 3)]

    NT = (((1,), (1,)), ((), ()))
    TN = (((0,), (0,)), ((), ()))
    for half in range(2):
        p0 = ends[half]
        t0, t1 = first_tiles[half], last_tiles[half]
        places = p0 + lax.broadcasted_iota(jnp.int32, (1, COLS), 1) % ROWS
        begin = start_of(places, starts)
        last_begin = start_of(p0 + ROWS - 1, starts)

        def stats_step(tile, carry):
            m, l, w = carry
            r0 = pl.multiple_of(tile * TILE, TILE)
            at = pl.multiple_of((tile - t0) * TILE, TILE)
            masks = tile_masks(r0)
            for which, dst in ((0, kc_ref), (1, vc_ref)):
                x = raw_window(which, r0)
                y = filters_ref[1 + which, 0:1] * x[0]
                for s in range(1, 3):
                    y = y + jnp.where(masks[s - 1], filters_ref[1 + which, s : s + 1] * x[s], 0.0)
                dst[pl.ds(r0, TILE)] = y.astype(BF16)
            s_ref[pl.ds(at, TILE)] = (
                lax.dot_general(kc_ref[pl.ds(r0, TILE)], qs_ref[half], NT, preferred_element_type=F32)
                * (SCALE * LOG2E)
            )

            @pl.when(jnp.logical_or(r0 < last_begin, r0 + TILE - 1 > p0))
            def _():
                keys = r0 + lax.broadcasted_iota(jnp.int32, (TILE, COLS), 0)
                allowed = jnp.logical_and(keys <= places, keys >= begin)
                s_ref[pl.ds(at, TILE)] = jnp.where(allowed, s_ref[pl.ds(at, TILE)], -1e30)

            dp_ref[pl.ds(at, TILE)] = (
                lax.dot_general(vc_ref[pl.ds(r0, TILE)], dos_ref[half], NT, preferred_element_type=F32)
                * SCALE
            )
            s = s_ref[pl.ds(at, TILE)].reshape(TILE // 8, 8, COLS)
            dp = dp_ref[pl.ds(at, TILE)].reshape(TILE // 8, 8, COLS)
            m_new = jnp.maximum(m, jnp.max(s, axis=0))
            factor = jnp.exp2(m - m_new)
            p = jnp.exp2(s - m_new[None])
            l = l * factor + jnp.sum(p, axis=0)
            w = w * factor + jnp.sum(p * dp, axis=0)
            return m_new, l, w

        m, l, w = lax.fori_loop(
            t0, t1, stats_step,
            (jnp.full((8, COLS), -1e30, F32), jnp.zeros((8, COLS), F32), jnp.zeros((8, COLS), F32)),
        )
        top = jnp.max(m, axis=0, keepdims=True)
        factor = jnp.exp2(m - top)
        total = jnp.sum(l * factor, axis=0, keepdims=True)
        lse = top + jnp.log2(total)
        mean = jnp.sum(w * factor, axis=0, keepdims=True) / total
        dqt_ref[...] = jnp.zeros((WIDTH, COLS), F32)

        def grads_step(tile, _):
            r0 = pl.multiple_of(tile * TILE, TILE)
            at = pl.multiple_of((tile - t0) * TILE, TILE)
            p = jnp.exp2(s_ref[pl.ds(at, TILE)] - lse)
            ds = (p * (dp_ref[pl.ds(at, TILE)] - mean)).astype(BF16)
            dv_ref[pl.ds(r0, TILE)] += jnp.dot(p.astype(BF16), dos_ref[half], preferred_element_type=F32)
            dk_ref[pl.ds(r0, TILE)] += jnp.dot(ds, qs_ref[half], preferred_element_type=F32)
            dqt_ref[...] += lax.dot_general(kc_ref[pl.ds(r0, TILE)], ds, TN, preferred_element_type=F32)
            return 0

        lax.fori_loop(t0, t1, grads_step, 0)
        dq = jnp.transpose(dqt_ref[...])
        masks = q_masks(half)
        sums = [jnp.zeros((8, WIDTH), F32) for _ in range(3)]
        for h in range(HEADS):
            grad = dq[h * ROWS : (h + 1) * ROWS]
            dq_ref[half, :, h * WIDTH : (h + 1) * WIDTH] = grad
            x = q_window(half, h)
            for s in range(3):
                term = grad * x[s]
                if s:
                    term = jnp.where(masks[s - 1], term, 0.0)
                sums[s] = sums[s] + jnp.sum(term.reshape(ROWS // 8, 8, WIDTH), axis=0)
        if half == 0:
            q_sums = sums
        else:
            q_sums = [a + b for a, b in zip(q_sums, sums)]

    def finish(tile, carry):
        r0 = pl.multiple_of(tile * TILE, TILE)
        inside = jnp.logical_or(
            jnp.logical_and(tile >= first_tiles[0], tile < last_tiles[0]),
            jnp.logical_and(tile >= first_tiles[1], tile < last_tiles[1]),
        )

        def full(carry):
            places = r0 + lax.broadcasted_iota(jnp.int32, (TILE, WIDTH), 0)
            begin = start_of(places, starts)
            masks = [places - s >= begin for s in range(1, 3)]
            ahead = [
                jnp.logical_and(places >= start_of(places + s, starts), places + s < LENGTH)
                for s in range(1, 3)
            ]
            nxt = pl.multiple_of(jnp.minimum(r0 + TILE, LENGTH - 8), 8)
            sums = []
            for which, acc in ((0, dk_ref), (1, dv_ref)):
                x = raw_window(which, r0)
                here = acc[pl.ds(r0, TILE)]
                cat = jnp.concatenate([here, acc[pl.ds(nxt, 8)]], axis=0)
                y = filters_ref[1 + which, 0:1] * here
                for s in range(1, 3):
                    y = y + jnp.where(
                        ahead[s - 1], filters_ref[1 + which, s : s + 1] * cat[s : s + TILE], 0.0
                    )
                out_ref[which, pl.ds(r0, TILE)] = y.astype(BF16)
                for s in range(3):
                    term = here * x[s]
                    if s:
                        term = jnp.where(masks[s - 1], term, 0.0)
                    sums.append(jnp.sum(term.reshape(TILE // 8, 8, WIDTH), axis=0))
            return tuple(a + b for a, b in zip(carry, sums))

        def blank(carry):
            for which in range(2):
                out_ref[which, pl.ds(r0, TILE)] = jnp.zeros((TILE, WIDTH), BF16)
            return carry

        return lax.cond(inside, full, blank, carry)

    sums = lax.fori_loop(0, N_TILES, finish, tuple(jnp.zeros((8, WIDTH), F32) for _ in range(6)))
    sums = list(q_sums) + list(sums)
    taps_ref[...] = jnp.zeros((16, WIDTH), F32)
    for i in range(9):
        taps_ref[i : i + 1] = jnp.sum(sums[i], axis=0, keepdims=True)


def attend(lengths, filters, q, rim, d_out, gathered):
    vmem = pl.BlockSpec(memory_space=pltpu.VMEM)
    return pl.pallas_call(
        attend_kernel,
        out_shape=(
            jax.ShapeDtypeStruct((2, ROWS, HEADS * WIDTH), F32),
            jax.ShapeDtypeStruct((2, LENGTH, WIDTH), BF16),
            jax.ShapeDtypeStruct((16, WIDTH), F32),
        ),
        in_specs=[pl.BlockSpec(memory_space=pltpu.SMEM)] + [vmem] * 5,
        out_specs=(vmem,) * 3,
        scratch_shapes=[
            pltpu.VMEM((LENGTH, WIDTH), BF16),
            pltpu.VMEM((LENGTH, WIDTH), BF16),
            pltpu.VMEM((MAX_TILES * TILE, COLS), F32),
            pltpu.VMEM((MAX_TILES * TILE, COLS), F32),
            pltpu.VMEM((LENGTH, WIDTH), F32),
            pltpu.VMEM((LENGTH, WIDTH), F32),
            pltpu.VMEM((2, COLS, WIDTH), BF16),
            pltpu.VMEM((2, COLS, WIDTH), BF16),
            pltpu.VMEM((WIDTH, COLS), F32),
        ],
        compiler_params=pltpu.CompilerParams(vmem_limit_bytes=56 << 20),
        name="attend",
    )(lengths, filters, q, rim, d_out, gathered)


def reduce_hops(n):
    if n == 2:
        return [[(1, 1, None)]]
    if n == 4:
        return [[(1, 2, None), (-1, -2, None)], [(1, 1, 0), (-1, -1, 1)]]
    return [
        [(1, 4, None), (-1, -4, None)],
        [(1, 3, 0), (-1, -3, 1)],
        [(1, 2, 2), (-1, -2, 2)],
        [(1, 1, 2), (-1, -1, 2)],
    ]


def scatter_kernel(
    lengths_ref, filters_ref, part_ref, dq_ref, taps_ref,
    dqp_ref, dkp_ref, dvp_ref, dfil_ref,
    *scratch,
):
    buffers = scratch[: 3 * len(PLAN)]
    sums = scratch[3 * len(PLAN) : 5 * len(PLAN)]
    rim_ref, tap_z, tap_x, tap_w, send_sem, recv_sem, rim_send, rim_recv, tap_send, tap_recv = scratch[
        5 * len(PLAN) :
    ]
    c = lax.axis_index("ctx")
    tp = lax.axis_index("tp")
    co = coords()
    after, before = (c + 1) % CTX, (c + CTX - 1) % CTX

    me_w = co[Y] * TP + tp
    peers = [
        [(shifted(co, Z, i), tp) for i in range(1, 8)],
        [(shifted(co, X, i), tp) for i in range(1, 4)],
        [],
    ]
    for i in range(1, 8):
        other = (me_w + i) % 8
        peers[2].append(([other // TP, co[X], co[Z]], other % TP))
    barrier = pltpu.get_barrier_semaphore()
    greet = [(ctx_of(place), core) for group in peers for place, core in group] + [(after, tp), (before, tp)]
    for ctx, core in greet:
        pl.semaphore_signal(barrier, inc=1, device_id={"ctx": ctx, "tp": core}, device_id_type=MESH)
    pl.semaphore_wait(barrier, len(greet))

    def send(src, dst, send_at, recv_at, ctx, core):
        copy = pltpu.make_async_remote_copy(
            src_ref=src, dst_ref=dst, send_sem=send_at, recv_sem=recv_at,
            device_id={"ctx": ctx, "tp": core}, device_id_type=MESH,
        )
        copy.start()
        return copy

    all_copies = []

    def start(chunk, hop):
        which, half, row, rows, order = PLAN[chunk]
        stage, entries, at_hop = hops[chunk][hop]
        dims = order[: 3 - stage]
        dim = dims[-1]
        kept = sorted(dims[:-1])
        started = []
        for i, (slot, direction, offset, had) in enumerate(entries):
            target = block_at(half, dim, shifted(co, dim, offset)[dim])

            def own(row_at, count):
                if stage == 0:
                    at = [pl.ds(0, SIZES[d]) for d in range(3)]
                    at[dim] = target
                    return part_ref.at[which, half, at[0], at[1], at[2], pl.ds(row + row_at, count)]
                at = [pl.ds(0, SIZES[d]) if d != dim else target for d in sorted(dims)]
                return sums[2 * chunk + stage - 1].at[(*at, pl.ds(row_at, count))]

            buffer = buffers[3 * chunk + stage]
            whole = tuple(pl.ds(0, SIZES[d]) for d in kept)
            half_rows = rows // 2
            first = at_hop == 0
            n_hops = len(reduce_hops(SIZES[dim]))
            lo, count = (i * half_rows, half_rows) if first and n_hops > 1 else (0, rows)
            if first:
                if stage == 0:
                    src = own(lo, count)
                else:
                    stash = buffer.at[(i, n_hops, *whole, pl.ds(lo, count))]
                    stash[...] = own(lo, count)[...].astype(BF16)
                    src = stash
            else:
                held = buffer.at[(i, at_hop - 1, *whole, pl.ds(0, rows))]
                if had == 2:
                    held[...] = (held[...].astype(F32) + own(0, rows)[...].astype(F32)).astype(BF16)
                else:
                    came = buffer.at[(i, at_hop - 1, *whole, pl.ds(had * half_rows, half_rows))]
                    rest = buffer.at[(i, at_hop - 1, *whole, pl.ds((1 - had) * half_rows, half_rows))]
                    came[...] = (
                        came[...].astype(F32) + own(had * half_rows, half_rows)[...].astype(F32)
                    ).astype(BF16)
                    rest[...] = own((1 - had) * half_rows, half_rows)[...].astype(BF16)
                src = held
            dst = buffer.at[(i, at_hop, *whole, pl.ds(lo, count))]
            started.append(
                send(
                    src, dst, send_sem.at[chunk, slot], recv_sem.at[chunk, slot],
                    ctx_of(shifted(co, dim, direction)), tp,
                )
            )
        all_copies.extend(started)
        return started

    def close_stage(chunk, stage):
        which, half, row, rows, order = PLAN[chunk]
        dims = order[: 3 - stage]
        dim = dims[-1]
        kept = sorted(dims[:-1])
        mine = block_at(half, dim, co[dim])
        buffer = buffers[3 * chunk + stage]
        if stage == 0:
            at = [pl.ds(0, SIZES[d]) for d in range(3)]
            at[dim] = mine
            total = part_ref[which, half, at[0], at[1], at[2], pl.ds(row, rows)].astype(F32)
        else:
            at = [pl.ds(0, SIZES[d]) if d != dim else mine for d in sorted(dims)]
            total = sums[2 * chunk + stage - 1][tuple(at)]
        last = len(reduce_hops(SIZES[dim])) - 1
        whole = tuple(pl.ds(0, SIZES[d]) for d in kept)
        for i in range(1 if SIZES[dim] == 2 else 2):
            total = total + buffer[(i, last, *whole)].astype(F32)
        if stage < 2:
            sums[2 * chunk + stage][...] = total
        else:
            out = dkp_ref if which == 0 else dvp_ref
            out[half, pl.ds(row, rows)] = total

    hops = []
    for plan in PLAN:
        steps, slot = [], 0
        for stage in range(3):
            for at_hop, hop in enumerate(reduce_hops(SIZES[plan[4][2 - stage]])):
                steps.append((stage, [(slot + i,) + entry for i, entry in enumerate(hop)], at_hop))
                slot += len(hop)
        hops.append(steps)

    tap_buffers = (tap_z, tap_x, tap_w)
    tap_me = (co[Z], co[X], me_w)
    tap_copies = []

    def tap_start(stage, value):
        buffer = tap_buffers[stage]
        mine = tap_me[stage]
        buffer[mine] = value
        started = []
        base = sum(len(p) for p in peers[:stage])
        for i, (place, core) in enumerate(peers[stage]):
            started.append(
                send(
                    buffer.at[mine], buffer.at[mine], tap_send.at[base + i], tap_recv.at[base + i],
                    ctx_of(place), core,
                )
            )
        tap_copies.extend(started)
        return started

    def tap_sum(stage, started):
        for copy in started:
            copy.wait_recv()
        buffer = tap_buffers[stage]
        total = buffer[0]
        for i in range(1, buffer.shape[0]):
            total = total + buffer[i]
        return total

    rims = [
        send(dq_ref.at[half, pl.ds(0, 8)], rim_ref.at[half], rim_send.at[half], rim_recv.at[half], target, tp)
        for half, target in ((0, before), (1, after))
    ]
    flying = [start(chunk, 0) for chunk in range(len(PLAN))]
    taps_flying = tap_start(0, taps_ref[...])

    for copy in rims:
        copy.wait_recv()
    starts = doc_starts(lengths_ref)
    for half in range(2):
        p0 = c * ROWS if half == 0 else (2 * CTX - 1 - c) * ROWS
        places = p0 + lax.broadcasted_iota(jnp.int32, (ROWS, WIDTH), 0)
        ahead = [
            jnp.logical_and(places >= start_of(places + s, starts), places + s < LENGTH) for s in range(1, 3)
        ]
        for h in range(HEADS):
            lanes = slice(h * WIDTH, (h + 1) * WIDTH)
            beyond = rim_ref[half, :, lanes]
            if half == 0:
                beyond = jnp.where(c == CTX - 1, dq_ref[1, 0:8, lanes], beyond)
            here = dq_ref[half, :, lanes]
            cat = jnp.concatenate([here, beyond], axis=0)
            y = filters_ref[0, 0:1] * here
            for s in range(1, 3):
                y = y + jnp.where(ahead[s - 1], filters_ref[0, s : s + 1] * cat[s : s + ROWS], 0.0)
            dqp_ref[half, :, lanes] = y

    n_hops = len(hops[0])
    for hop in range(1, n_hops + 1):
        for chunk in range(len(PLAN)):
            for copy in flying[chunk]:
                copy.wait_recv()
            stage = hops[chunk][hop - 1][0]
            if hop == n_hops or hops[chunk][hop][0] != stage:
                close_stage(chunk, stage)
            if hop < n_hops:
                flying[chunk] = start(chunk, hop)
        if hop in (2, 4):
            taps_flying = tap_start(hop // 2, tap_sum(hop // 2 - 1, taps_flying))
    dfil_ref[...] = tap_sum(2, taps_flying)
    for copy in all_copies + tap_copies + rims:
        copy.wait_send()


def scatter(lengths, filters, part, dq, taps):
    vmem = pl.BlockSpec(memory_space=pltpu.VMEM)
    buffers, sums = [], []
    for _, _, _, rows, order in PLAN:
        for stage in range(3):
            dims = order[: 3 - stage]
            kept = tuple(SIZES[d] for d in sorted(dims[:-1]))
            n = SIZES[dims[-1]]
            steps = len(reduce_hops(n)) + (1 if stage else 0)
            buffers.append(pltpu.VMEM((1 if n == 2 else 2, steps) + kept + (rows, WIDTH), BF16))
            if stage < 2:
                sums.append(pltpu.VMEM(kept + (rows, WIDTH), F32))
    return pl.pallas_call(
        scatter_kernel,
        out_shape=(
            jax.ShapeDtypeStruct((2, ROWS, HEADS * WIDTH), F32),
            jax.ShapeDtypeStruct((2, ROWS, WIDTH), F32),
            jax.ShapeDtypeStruct((2, ROWS, WIDTH), F32),
            jax.ShapeDtypeStruct((16, WIDTH), F32),
        ),
        in_specs=[pl.BlockSpec(memory_space=pltpu.SMEM)] + [vmem] * 4,
        out_specs=(vmem,) * 4,
        scratch_shapes=buffers
        + sums
        + [
            pltpu.VMEM((2, 8, HEADS * WIDTH), F32),
            pltpu.VMEM((8, 16, WIDTH), F32),
            pltpu.VMEM((4, 16, WIDTH), F32),
            pltpu.VMEM((8, 16, WIDTH), F32),
            pltpu.SemaphoreType.DMA((len(PLAN), SLOTS)),
            pltpu.SemaphoreType.DMA((len(PLAN), SLOTS)),
            pltpu.SemaphoreType.DMA((2,)),
            pltpu.SemaphoreType.DMA((2,)),
            pltpu.SemaphoreType.DMA((17,)),
            pltpu.SemaphoreType.DMA((17,)),
        ],
        compiler_params=pltpu.CompilerParams(
            collective_id=2, has_side_effects=True, vmem_limit_bytes=40 << 20
        ),
        name="scatter",
    )(lengths, filters, part, dq, taps)


def shards(q_pre, k_pre, value_before_filter, d_out, filters, doc_lengths):
    gathered, rim = gather(k_pre, value_before_filter, q_pre)
    dq, part, taps = attend(
        doc_lengths, filters, q_pre, rim, d_out, gathered.reshape(2, LENGTH, WIDTH)
    )
    part = part.reshape((2, 2) + SIZES + (ROWS, WIDTH))
    d_q, d_k, d_v, d_filters = scatter(doc_lengths, filters, part, dq, taps)
    return d_q, d_k, d_v, d_filters[:9].reshape(3, 3, WIDTH)


def solution(mesh):
    split = P(None, "ctx", "tp")
    return jax.shard_map(
        shards,
        mesh=mesh,
        in_specs=(split, split, split, split, P(), P()),
        out_specs=(split, split, split, P()),
        check_vma=False,
    )
```

```python
import math

import jax
import jax.numpy as jnp
from jax import lax
from jax.experimental import pallas as pl
from jax.experimental.pallas import tpu as pltpu
from jax.sharding import PartitionSpec as P

MESH = pl.DeviceIdType.MESH
Y, X, Z = 0, 1, 2
SIZES = (2, 4, 8)
CTX = 64
TP = 4
ROWS = 64
LENGTH = 8192
HEADS = 8
WIDTH = 128
COLS = HEADS * ROWS
TILE = 512
N_TILES = LENGTH // TILE
MAX_TILES = (2 * (TILE - 1) + LENGTH // 2 + ROWS - 1) // TILE
SCALE = WIDTH ** (-0.5)
LOG2E = math.log2(math.e)
F32 = jnp.float32
BF16 = jnp.bfloat16

GATHER_PLAN = (
    (0, 0, 0, 64, (Y, X, Z), ("pair", "all4", "ring8")),
    (1, 1, 0, 64, (Y, Z, X), ("pair", "two8", "ring4")),
    (0, 1, 0, 64, (X, Z, Y), ("all4", "ring8", "pair")),
    (1, 0, 0, 64, (Z, X, Y), ("all8", "ring4", "pair")),
)
SCATTER_PLAN = (
    (0, 0, 0, 64, (Y, X, Z), ("pair", "ring4", "ring8")),
    (1, 1, 0, 64, (Y, X, Z), ("pair", "ring4", "ring8")),
    (0, 1, 0, 64, (Z, X, Y), ("ring8", "ring4", "pair")),
    (1, 0, 0, 64, (Z, Y, X), ("ring8", "pair", "ring4")),
)

WAYS = {
    "pair": ((1, 0, None, None),),
    "ring4": ((1, 0, None, None), (-1, 0, None, None), (1, -1, 0, 0), (-1, 1, 1, 1)),
    "all4": ((2, 0, None, None), (1, 0, None, None), (-1, 0, None, None)),
    "ring8": (
        (1, 0, None, None), (-1, 0, None, None), (1, -1, None, 0), (-1, 1, None, 1),
        (1, -2, None, 2), (-1, 2, None, 3), (1, -3, 0, 4), (-1, 3, 1, 5),
    ),
    "three8": (
        (2, 0, None, None), (-2, 0, None, None), (1, 0, None, None), (-1, 0, None, None),
        (1, -2, None, 0), (-1, 2, None, 1), (1, -3, 0, 4), (-1, 3, 1, 5),
    ),
    "two8": (
        (2, 0, None, None), (-2, 0, None, None), (1, 0, None, None), (-1, 0, None, None),
        (2, -2, 0, 0), (-2, 2, 1, 1), (1, -2, None, 0), (-1, 2, None, 1),
    ),
    "all8": (
        (4, 0, None, None), (3, 0, None, None), (-3, 0, None, None), (2, 0, None, None), (-2, 0, None, None),
        (1, 0, None, None), (-1, 0, None, None),
    ),
}

LINK, LATENCY, FURTHER, ISSUE, ADD = 54e3, 2.1, 0.6, 0.06, 0.0003
ROW_BYTES = WIDTH * 2


def displacements(steps):
    found = {(s.link[0], far % SIZES[s.link[0]]) for s in steps if s.link for far in (s.link[1], -s.link[1])}
    return sorted(found)


def count_of(dims):
    return math.prod(SIZES[d] for d in dims)


class Step:
    def __init__(self, chunk, after=(), needs=(), link=None, blocks=0.0, adds=0.0, **what):
        self.chunk, self.after, self.needs, self.link = chunk, list(after), list(needs), link
        self.blocks, self.adds = blocks, adds
        self.__dict__.update(what)


def gather_steps(plan):
    steps = []

    def add(*args, **what):
        steps.append(Step(*args, **what))
        return len(steps) - 1

    for chunk, (_, _, _, rows, order, ways) in enumerate(plan):
        by_stage = []
        for stage, dim in enumerate(order):
            region = {d: None if s < stage else 0 for s, d in enumerate(order)}
            bundle = rows * count_of(order[:stage])
            here = []
            if stage == 2 and SIZES[dim] == 2:
                axis = order[1]
                region[axis] = 0
                here.append(
                    add(chunk, by_stage[0], link=(dim, 1), blocks=bundle / SIZES[axis], region=region, part=None)
                )
                for i in by_stage[1]:
                    there = dict(region)
                    there[axis] = steps[i].region[axis] - steps[i].link[1]
                    here.append(
                        add(chunk, [i], link=(dim, 1), blocks=steps[i].blocks, region=there, part=steps[i].part)
                    )
            else:
                for far, offset, part, first in WAYS[ways[stage]]:
                    there = dict(region)
                    there[dim] = offset
                    after = [here[first]] if first is not None else by_stage[-1] if stage else []
                    here.append(
                        add(
                            chunk, after, link=(dim, far), blocks=bundle * (1 if part is None else 0.5),
                            region=there, part=part,
                        )
                    )
            by_stage.append(here)
    return steps


def scatter_steps(plan):
    steps = []

    def add(*args, **what):
        steps.append(Step(*args, **what))
        return len(steps) - 1

    for chunk, (_, _, _, rows, order, ways) in enumerate(plan):
        ready = None
        for stage in range(3):
            dim = order[2 - stage]
            n = SIZES[dim]
            bundle = rows * count_of(order[: 2 - stage])
            if stage == 0 and n == 2:
                axis = order[1]
                m = SIZES[axis]
                ready = {}
                offsets = [m // 2] + [sign * o for o in range(m // 2 - 1, 0, -1) for sign in (1, -1)] + [0]
                for piece, offset in enumerate(offsets):
                    what = dict(stage=0, piece=piece, offset=offset)
                    i = add(chunk, link=(dim, 1), blocks=bundle / m, kind="piece", **what)
                    ready[offset % m] = add(chunk, [i], adds=bundle / m, kind="close_piece", **what)
                continue

            def own(offset):
                return [] if ready is None else [ready[offset % n if len(ready) > 1 else 0]]

            way = WAYS[ways[2 - stage]]
            made = {}
            for e in reversed(range(len(way))):
                far, offset, part, _ = way[e]
                inner = [k for k in range(len(way)) if way[k][3] == e]
                made[e] = add(
                    chunk, [made[k] for k in inner], own(offset - far), link=(dim, -far),
                    blocks=bundle * (1 if part is None else 0.5), adds=bundle if stage or inner else 0,
                    kind="send", stage=stage, entry=e, inner=inner, offset=offset - far, part=part,
                )
            outer = [k for k in range(len(way)) if way[k][3] is None]
            ready = {
                0: add(
                    chunk, [made[k] for k in outer], own(0), adds=bundle * len(outer),
                    kind="close", stage=stage, outer=outer,
                )
            }
    return steps


def in_order(steps):
    left = [len(s.after) + len(s.needs) for s in steps]
    users = [[] for _ in steps]
    for i, s in enumerate(steps):
        for j in s.after + s.needs:
            users[j].append(i)

    def wire(s):
        return abs(s.link[1]) * s.blocks * ROW_BYTES / LINK

    def late(s):
        return LATENCY + FURTHER * (abs(s.link[1]) - 1)

    rest = [0.0] * len(steps)
    for i in reversed(range(len(steps))):
        s = steps[i]
        own = ISSUE + s.adds * ADD + (wire(s) + late(s) if s.link else 0.0)
        rest[i] = own + max([rest[u] for u in users[i]], default=0.0)
    ready = [(0.0, -rest[i], i) for i in range(len(steps)) if left[i] == 0]
    when = [0.0] * len(steps)
    order, times, busy, now = [], [], {}, 0.0
    while ready:
        now = max(now, min(ready)[0])
        pick = min((r for r in ready if r[0] <= now), key=lambda r: r[1:])
        ready.remove(pick)
        i = pick[2]
        s = steps[i]
        order.append(i)
        times.append(now)
        now += ISSUE + s.adds * ADD
        seen = now
        if s.link:
            link = (s.link[0], s.link[1] > 0)
            busy[link] = max(now, busy.get(link, 0.0)) + wire(s)
            seen = busy[link] + late(s)
        for u in users[i]:
            when[u] = max(when[u], seen if i in steps[u].after else now)
            left[u] -= 1
            if left[u] == 0:
                ready.append((when[u], -rest[u], u))
    return order, times
def coords():
    c = lax.axis_index("ctx")
    return [c // 32, (c // 8) % 4, c % 8]


def ctx_of(co):
    return co[0] * 32 + co[1] * 8 + co[2]


def shifted(co, dim, by):
    co = list(co)
    co[dim] = (co[dim] + by + SIZES[dim]) % SIZES[dim]
    return co


def block_at(half, dim, at):
    return at if half == 0 else SIZES[dim] - 1 - at


def gather_kernel(k_ref, v_ref, q_ref, g_ref, rim_ref, send_sem, recv_sem, rim_send, rim_recv, own_sem):
    c = lax.axis_index("ctx")
    co = coords()
    after, before = (c + 1) % CTX, (c + CTX - 1) % CTX
    steps = gather_steps(GATHER_PLAN)
    neighbours = [ctx_of(shifted(co, *to)) for to in displacements(steps)] + [after, before]
    barrier = pltpu.get_barrier_semaphore()
    for neighbour in neighbours:
        pl.semaphore_signal(barrier, inc=1, device_id={"ctx": neighbour}, device_id_type=MESH)
    own = []
    for half in range(2):
        at = [block_at(half, d, co[d]) for d in range(3)]
        for which, source in ((0, k_ref), (1, v_ref)):
            copy = pltpu.make_async_copy(
                source.at[half], g_ref.at[which, half, at[0], at[1], at[2]], own_sem.at[which, half]
            )
            copy.start()
            own.append(copy)
    for copy in own:
        copy.wait()
    pl.semaphore_wait(barrier, len(neighbours))

    order, _ = in_order(steps)
    copies, rims, seen = {}, [], set()
    for n, i in enumerate(order):
        s = steps[i]
        for j in s.after:
            if j not in seen:
                copies[j].wait_recv()
                seen.add(j)
        which, half, row, rows, _, _ = GATHER_PLAN[s.chunk]
        at = []
        for d in range(3):
            if s.region[d] is None:
                at.append(pl.ds(0, SIZES[d]))
            else:
                at.append(block_at(half, d, shifted(co, d, s.region[d])[d]))
        if s.part is not None:
            rows = rows // 2
            row = row + s.part * rows
        ref = g_ref.at[which, half, at[0], at[1], at[2], pl.ds(row, rows)]
        copies[i] = pltpu.make_async_remote_copy(
            src_ref=ref,
            dst_ref=ref,
            send_sem=send_sem.at[i],
            recv_sem=recv_sem.at[i],
            device_id={"ctx": ctx_of(shifted(co, *s.link))},
            device_id_type=MESH,
        )
        copies[i].start()
        if n == len(order) // 4:
            for side, target in ((0, after), (1, before)):
                copy = pltpu.make_async_remote_copy(
                    src_ref=q_ref.at[side, pl.ds(ROWS - 16, 16)],
                    dst_ref=rim_ref.at[side],
                    send_sem=rim_send.at[side],
                    recv_sem=rim_recv.at[side],
                    device_id={"ctx": target},
                    device_id_type=MESH,
                )
                copy.start()
                rims.append(copy)
    for i in order:
        if i not in seen:
            copies[i].wait_recv()
    for copy in rims:
        copy.wait()
    for i in order:
        copies[i].wait_send()


def gather(k, v, q):
    count = len(gather_steps(GATHER_PLAN))
    hbm = pl.BlockSpec(memory_space=pltpu.HBM)
    return pl.pallas_call(
        gather_kernel,
        out_shape=(
            jax.ShapeDtypeStruct((2, 2) + SIZES + (ROWS, WIDTH), BF16),
            jax.ShapeDtypeStruct((2, 16, HEADS * WIDTH), BF16),
        ),
        in_specs=[hbm] * 3,
        out_specs=(hbm,) * 2,
        scratch_shapes=[
            pltpu.SemaphoreType.DMA((count,)),
            pltpu.SemaphoreType.DMA((count,)),
            pltpu.SemaphoreType.DMA((2,)),
            pltpu.SemaphoreType.DMA((2,)),
            pltpu.SemaphoreType.DMA((2, 2)),
        ],
        compiler_params=pltpu.CompilerParams(
            collective_id=1, has_side_effects=True, vmem_limit_bytes=60 << 20
        ),
        name="gather",
    )(k, v, q)


def doc_starts(lengths_ref):
    starts = [jnp.int32(0)]
    for d in range(7):
        starts.append(starts[-1] + lengths_ref[d])
    return starts


def start_of(places, starts):
    found = jnp.zeros_like(places)
    for s in starts[1:]:
        found = jnp.where(places >= s, s, found)
    return found


def attend_kernel(
    lengths_ref, filters_ref, q_hbm, rim_hbm, do_hbm, g_hbm,
    dq_ref, out_hbm, taps_ref,
    q_ref, rim_ref, do_ref, raw_ref, kc_ref, vc_ref, s_ref, dp_ref, dk_ref, dv_ref, qs_ref, dos_ref, dqt_ref,
    zero_ref, tap_ref, in_sem, tile_sem, out_sem,
):
    c = lax.axis_index("ctx")
    starts = doc_starts(lengths_ref)
    ends = (c * ROWS, (2 * CTX - 1 - c) * ROWS)
    heads, tails = [], []
    for half in range(2):
        heads.append(start_of(ends[half], starts) // TILE)
        tails.append((ends[half] + ROWS + TILE - 1) // TILE)
    spans = ((heads[0], tails[0]), (jnp.maximum(heads[1], tails[0]), tails[1]))

    def inside(tile):
        return jnp.logical_or(
            jnp.logical_and(tile >= heads[0], tile < tails[0]),
            jnp.logical_and(tile >= heads[1], tile < tails[1]),
        )

    def row_of(tile):
        return pl.multiple_of(tile * TILE, TILE)

    def over_spans(fn):
        for lo, hi in spans:
            lax.fori_loop(lo, hi, lambda tile, _: (fn(tile), 0)[1], 0)

    loads = [
        pltpu.make_async_copy(src, dst, in_sem.at[i])
        for i, (src, dst) in enumerate(((q_hbm, q_ref), (rim_hbm, rim_ref), (do_hbm, do_ref)))
    ]
    for copy in loads:
        copy.start()

    def tile_load(which, tile):
        rows = pl.ds(row_of(tile), TILE)
        return pltpu.make_async_copy(g_hbm.at[which, rows], raw_ref.at[which, rows], tile_sem.at[which, tile])

    def tile_store(which, tile, src):
        return pltpu.make_async_copy(src, out_hbm.at[which, pl.ds(row_of(tile), TILE)], out_sem.at[which, tile])

    def start_load(tile):
        for which in range(2):
            tile_load(which, tile).start()

    over_spans(start_load)
    zero_ref[...] = jnp.zeros((TILE, WIDTH), BF16)

    def over_blank(act):
        def body(tile, _):
            @pl.when(jnp.logical_not(inside(tile)))
            def _():
                for which in range(2):
                    act(tile_store(which, tile, zero_ref))

            return 0

        lax.fori_loop(0, N_TILES, body, 0)

    over_blank(lambda copy: copy.start())
    for copy in loads:
        copy.wait()

    def q_window(half, h):
        lanes = slice(h * WIDTH, (h + 1) * WIDTH)
        before = rim_ref[half, :, lanes]
        if half == 1:
            before = jnp.where(c == CTX - 1, q_ref[0, ROWS - 16 :, lanes], before)
        cat = jnp.concatenate([before.astype(F32), q_ref[half, :, lanes].astype(F32)], axis=0)
        return [cat[16 - s : 16 - s + ROWS] for s in range(3)]

    def q_masks(half):
        places = ends[half] + lax.broadcasted_iota(jnp.int32, (ROWS, WIDTH), 0)
        begin = start_of(places, starts)
        return [places - s >= begin for s in range(1, 3)]

    for half in range(2):
        masks = q_masks(half)
        for h in range(HEADS):
            x = q_window(half, h)
            y = filters_ref[0, 0:1] * x[0]
            for s in range(1, 3):
                y = y + jnp.where(masks[s - 1], filters_ref[0, s : s + 1] * x[s], 0.0)
            qs_ref[half, h * ROWS : (h + 1) * ROWS] = y.astype(BF16)
            dos_ref[half, h * ROWS : (h + 1) * ROWS] = do_ref[half, :, h * WIDTH : (h + 1) * WIDTH]

    def raw_window(which, tile):
        r0 = row_of(tile)
        before = raw_ref[which, pl.ds(pl.multiple_of(jnp.maximum(r0 - 16, 0), 16), 16)].astype(F32)
        first = jnp.logical_or(tile == heads[0], jnp.logical_and(tile == heads[1], heads[1] >= tails[0]))
        before = jnp.where(first, 0.0, before)
        cat = jnp.concatenate([before, raw_ref[which, pl.ds(r0, TILE)].astype(F32)], axis=0)
        return [cat[16 - s : 16 - s + TILE] for s in range(3)]

    def has_edge(tile):
        r0 = row_of(tile)
        found = jnp.logical_or(tile == 0, tile == N_TILES - 1)
        for s in starts[1:]:
            found = jnp.logical_or(found, jnp.logical_and(s >= r0 - 1, s <= r0 + TILE + 1))
        return found

    def both_ways(tile, fn):
        edge = has_edge(tile)

        @pl.when(edge)
        def _():
            places = row_of(tile) + lax.broadcasted_iota(jnp.int32, (TILE, WIDTH), 0)
            fn(tile, places)

        @pl.when(jnp.logical_not(edge))
        def _():
            fn(tile, None)

    def masked(mask, value):
        return value if mask is None else jnp.where(mask, value, 0.0)

    def back_masks(places):
        if places is None:
            return [None, None, None]
        begin = start_of(places, starts)
        return [None] + [places - s >= begin for s in range(1, 3)]

    def ahead_masks(places):
        if places is None:
            return [None, None, None]
        return [None] + [
            jnp.logical_and(places >= start_of(places + s, starts), places + s < LENGTH) for s in range(1, 3)
        ]

    def convolve(tile, places):
        masks = back_masks(places)
        r0 = row_of(tile)
        for which, dst in ((0, kc_ref), (1, vc_ref)):
            x = raw_window(which, tile)
            y = filters_ref[1 + which, 0:1] * x[0]
            for s in range(1, 3):
                y = y + masked(masks[s], filters_ref[1 + which, s : s + 1] * x[s])
            dst[pl.ds(r0, TILE)] = y.astype(BF16)

    def prepare(tile):
        for which in range(2):
            tile_load(which, tile).wait()
        both_ways(tile, convolve)
        r0 = row_of(tile)
        dk_ref[pl.ds(r0, TILE)] = jnp.zeros((TILE, WIDTH), F32)
        dv_ref[pl.ds(r0, TILE)] = jnp.zeros((TILE, WIDTH), F32)

    over_spans(prepare)

    NT = (((1,), (1,)), ((), ()))
    TN = (((0,), (0,)), ((), ()))
    for half in range(2):
        p0 = ends[half]
        t0, t1 = heads[half], tails[half]
        places = p0 + lax.broadcasted_iota(jnp.int32, (1, COLS), 1) % ROWS
        begin = start_of(places, starts)
        last_begin = start_of(p0 + ROWS - 1, starts)

        def stats_step(tile, carry, edge):
            m, l, w = carry
            r0 = row_of(tile)
            at = row_of(tile - t0)
            s = (
                lax.dot_general(kc_ref[pl.ds(r0, TILE)], qs_ref[half], NT, preferred_element_type=F32)
                * (SCALE * LOG2E)
            )
            if edge:
                keys = r0 + lax.broadcasted_iota(jnp.int32, (TILE, COLS), 0)
                s = jnp.where(jnp.logical_and(keys <= places, keys >= begin), s, -1e30)
            s_ref[pl.ds(at, TILE)] = s
            dp = (
                lax.dot_general(vc_ref[pl.ds(r0, TILE)], dos_ref[half], NT, preferred_element_type=F32)
                * SCALE
            )
            dp_ref[pl.ds(at, TILE)] = dp
            s = s.reshape(TILE // 8, 8, COLS)
            dp = dp.reshape(TILE // 8, 8, COLS)
            m_new = jnp.maximum(m, jnp.max(s, axis=0))
            factor = jnp.exp2(m - m_new)
            p = jnp.exp2(s - m_new[None])
            l = l * factor + jnp.sum(p, axis=0)
            w = w * factor + jnp.sum(p * dp, axis=0)
            return m_new, l, w

        carry = (jnp.full((8, COLS), -1e30, F32), jnp.zeros((8, COLS), F32), jnp.zeros((8, COLS), F32))
        e0 = jnp.minimum((last_begin + TILE - 1) // TILE, t1)
        e1 = jnp.maximum(e0, (p0 + 1) // TILE)
        for lo, hi, edge in ((t0, e0, True), (e0, e1, False), (e1, t1, True)):
            carry = lax.fori_loop(lo, hi, lambda tile, carry, edge=edge: stats_step(tile, carry, edge), carry)
        m, l, w = carry
        top = jnp.max(m, axis=0, keepdims=True)
        factor = jnp.exp2(m - top)
        total = jnp.sum(l * factor, axis=0, keepdims=True)
        lse = top + jnp.log2(total)
        mean = jnp.sum(w * factor, axis=0, keepdims=True) / total
        dqt_ref[...] = jnp.zeros((WIDTH, COLS), F32)

        def grads_step(tile, _):
            r0 = row_of(tile)
            at = row_of(tile - t0)
            p = jnp.exp2(s_ref[pl.ds(at, TILE)] - lse)
            ds = (p * (dp_ref[pl.ds(at, TILE)] - mean)).astype(BF16)
            dv_ref[pl.ds(r0, TILE)] += jnp.dot(p.astype(BF16), dos_ref[half], preferred_element_type=F32)
            dk_ref[pl.ds(r0, TILE)] += jnp.dot(ds, qs_ref[half], preferred_element_type=F32)
            dqt_ref[...] += lax.dot_general(kc_ref[pl.ds(r0, TILE)], ds, TN, preferred_element_type=F32)
            return 0

        lax.fori_loop(t0, t1, grads_step, 0)
        dq = jnp.transpose(dqt_ref[...])
        masks = q_masks(half)
        sums = [jnp.zeros((8, WIDTH), F32) for _ in range(3)]
        for h in range(HEADS):
            grad = dq[h * ROWS : (h + 1) * ROWS]
            dq_ref[half, :, h * WIDTH : (h + 1) * WIDTH] = grad
            x = q_window(half, h)
            for s in range(3):
                term = grad * x[s]
                if s:
                    term = jnp.where(masks[s - 1], term, 0.0)
                sums[s] = sums[s] + jnp.sum(term.reshape(ROWS // 8, 8, WIDTH), axis=0)
        for s in range(3):
            tap_ref[s] = sums[s] if half == 0 else tap_ref[s] + sums[s]

    tap_ref[3:9] = jnp.zeros((6, 8, WIDTH), F32)

    def finish(tile, places):
        back, ahead = back_masks(places), ahead_masks(places)
        r0 = row_of(tile)
        beyond = pl.ds(pl.multiple_of(jnp.minimum(r0 + TILE, LENGTH - 8), 8), 8)
        more = inside(tile + 1)
        for which, acc, stage in ((0, dk_ref, kc_ref), (1, dv_ref, vc_ref)):
            x = raw_window(which, tile)
            here = acc[pl.ds(r0, TILE)]
            cat = jnp.concatenate([here, jnp.where(more, acc[beyond], 0.0)], axis=0)
            y = filters_ref[1 + which, 0:1] * here
            for s in range(1, 3):
                y = y + masked(ahead[s], filters_ref[1 + which, s : s + 1] * cat[s : s + TILE])
            stage[pl.ds(r0, TILE)] = y.astype(BF16)
            for s in range(3):
                term = masked(back[s], here * x[s])
                tap_ref[3 + 3 * which + s] += jnp.sum(term.reshape(TILE // 8, 8, WIDTH), axis=0)

    def staged(which, tile):
        return (kc_ref, vc_ref)[which].at[pl.ds(row_of(tile), TILE)]

    def finish_tile(tile):
        both_ways(tile, finish)
        for which in range(2):
            tile_store(which, tile, staged(which, tile)).start()

    over_spans(finish_tile)
    taps_ref[...] = jnp.zeros((16, WIDTH), F32)
    for i in range(9):
        taps_ref[i : i + 1] = jnp.sum(tap_ref[i], axis=0, keepdims=True)

    def wait_store(tile):
        for which in range(2):
            tile_store(which, tile, staged(which, tile)).wait()

    over_spans(wait_store)
    over_blank(lambda copy: copy.wait())


def attend(lengths, filters, q, rim, d_out, gathered):
    vmem = pl.BlockSpec(memory_space=pltpu.VMEM)
    hbm = pl.BlockSpec(memory_space=pltpu.HBM)
    return pl.pallas_call(
        attend_kernel,
        out_shape=(
            jax.ShapeDtypeStruct((2, ROWS, HEADS * WIDTH), F32),
            jax.ShapeDtypeStruct((2, LENGTH, WIDTH), BF16),
            jax.ShapeDtypeStruct((16, WIDTH), F32),
        ),
        in_specs=[pl.BlockSpec(memory_space=pltpu.SMEM), vmem] + [hbm] * 4,
        out_specs=(vmem, hbm, vmem),
        scratch_shapes=[
            pltpu.VMEM((2, ROWS, HEADS * WIDTH), BF16),
            pltpu.VMEM((2, 16, HEADS * WIDTH), BF16),
            pltpu.VMEM((2, ROWS, HEADS * WIDTH), BF16),
            pltpu.VMEM((2, LENGTH, WIDTH), BF16),
            pltpu.VMEM((LENGTH, WIDTH), BF16),
            pltpu.VMEM((LENGTH, WIDTH), BF16),
            pltpu.VMEM((MAX_TILES * TILE, COLS), F32),
            pltpu.VMEM((MAX_TILES * TILE, COLS), F32),
            pltpu.VMEM((LENGTH, WIDTH), F32),
            pltpu.VMEM((LENGTH, WIDTH), F32),
            pltpu.VMEM((2, COLS, WIDTH), BF16),
            pltpu.VMEM((2, COLS, WIDTH), BF16),
            pltpu.VMEM((WIDTH, COLS), F32),
            pltpu.VMEM((TILE, WIDTH), BF16),
            pltpu.VMEM((9, 8, WIDTH), F32),
            pltpu.SemaphoreType.DMA((3,)),
            pltpu.SemaphoreType.DMA((2, N_TILES)),
            pltpu.SemaphoreType.DMA((2, N_TILES)),
        ],
        compiler_params=pltpu.CompilerParams(vmem_limit_bytes=60 << 20),
        name="attend",
    )(lengths, filters, q, rim, d_out, gathered)


def scatter_kernel(
    lengths_ref, filters_ref, part_hbm, dq_hbm, taps_hbm,
    dqp_ref, dkp_ref, dvp_ref, dfil_ref,
    *scratch,
):
    n_chunks = len(SCATTER_PLAN)
    came = scratch[: 3 * n_chunks]
    stash = scratch[3 * n_chunks : 6 * n_chunks]
    sums = scratch[6 * n_chunks : 8 * n_chunks]
    (
        part_ref, dq_ref, rim_ref, tap_in, tap_out,
        send_sem, recv_sem, rim_send, rim_recv, tap_send, tap_recv, part_sem,
    ) = scratch[8 * n_chunks :]
    c = lax.axis_index("ctx")
    tp = lax.axis_index("tp")
    co = coords()
    after, before = (c + 1) % CTX, (c + CTX - 1) % CTX
    steps = scatter_steps(SCATTER_PLAN)

    def flipped(value, bit):
        return value + bit - 2 * bit * ((value // bit) % 2)

    partners = []
    for dim, bit in ((Z, 1), (Z, 2), (Z, 4), (X, 1), (X, 2), (Y, 1)):
        place = list(co)
        place[dim] = flipped(co[dim], bit)
        partners.append((ctx_of(place), tp))
    partners += [(c, flipped(tp, 1)), (c, flipped(tp, 2))]
    near = set(displacements(steps)) | {(Z, 1), (Z, 7), (Z, 2), (Z, 6), (Z, 4), (X, 1), (X, 3), (X, 2), (Y, 1)}
    greet = [(ctx_of(shifted(co, *to)), tp) for to in sorted(near)]
    greet += [(after, tp), (before, tp)] + partners[-2:]
    barrier = pltpu.get_barrier_semaphore()
    for ctx, core in greet:
        pl.semaphore_signal(barrier, inc=1, device_id={"ctx": ctx, "tp": core}, device_id_type=MESH)
    loads = [
        pltpu.make_async_copy(part_hbm.at[which, half], part_ref.at[which, half], part_sem.at[2 * which + half])
        for which in range(2)
        for half in range(2)
    ]
    loads.append(pltpu.make_async_copy(dq_hbm, dq_ref, part_sem.at[4]))
    loads.append(pltpu.make_async_copy(taps_hbm, tap_out.at[0], part_sem.at[5]))
    for copy in loads:
        copy.start()
    pl.semaphore_wait(barrier, len(greet))

    def send(src, dst, send_at, recv_at, ctx, core):
        copy = pltpu.make_async_remote_copy(
            src_ref=src, dst_ref=dst, send_sem=send_at, recv_sem=recv_at,
            device_id={"ctx": ctx, "tp": core}, device_id_type=MESH,
        )
        copy.start()
        return copy

    loaded = set()

    def load(i):
        if i not in loaded:
            loads[i].wait()
            loaded.add(i)

    def blocks(dims, fn):
        sizes = [SIZES[d] for d in dims]

        def body(i, _):
            at = []
            for size in reversed(sizes):
                at.append(i % size)
                i = i // size
            fn(tuple(reversed(at)))
            return 0

        if sizes:
            lax.fori_loop(0, math.prod(sizes), body, 0)
        else:
            fn(())

    def own_at(s, target):
        which, half, row0, _, order, _ = SCATTER_PLAN[s.chunk]
        dim = order[2 - s.stage]
        kept = sorted(order[: 2 - s.stage])
        dims = sorted(order[: 3 - s.stage])
        if s.stage == 0:
            load(2 * which + half)

        def value(at, row, count):
            where = dict(zip(kept, at))
            where[dim] = target
            full = tuple(where[d] for d in dims)
            if s.stage == 0:
                return part_ref[(which, half, *full, pl.ds(row0 + row, count))].astype(F32)
            return sums[2 * s.chunk + s.stage - 1][(*full, pl.ds(row, count))]

        return value

    def run_send(i, s):
        which, half, row0, rows, order, ways = SCATTER_PLAN[s.chunk]
        dim = order[2 - s.stage]
        kept = sorted(order[: 2 - s.stage])
        whole = tuple(pl.ds(0, SIZES[d]) for d in kept)
        target = block_at(half, dim, shifted(co, dim, s.offset)[dim])
        arrived = came[3 * s.chunk + s.stage]
        mid = rows // 2
        row, count = (0, rows) if s.part is None else (s.part * mid, mid)
        if s.stage == 0 and not s.inner:
            where = [pl.ds(0, SIZES[d]) for d in range(3)]
            where[dim] = target
            src = part_hbm.at[(which, half, *where, pl.ds(row0 + row, count))]
        else:
            held = stash[3 * s.chunk + s.stage]
            own = own_at(s, target)
            way = WAYS[ways[2 - s.stage]]
            split = s.part is None and any(way[k][2] is not None for k in s.inner)

            def merge(at):
                for part in (0, 1) if split else (None,):
                    lo, n = (part * mid, mid) if split else (row, count)
                    value = own(at, lo, n)
                    for k in s.inner:
                        if not split or way[k][2] in (None, part):
                            value = value + arrived[(k, *at, pl.ds(lo, n))].astype(F32)
                    held[(s.entry, *at, pl.ds(lo, n))] = value.astype(BF16)

            blocks(kept, merge)
            src = held.at[(s.entry, *whole, pl.ds(row, count))]
        dst = arrived.at[(s.entry, *whole, pl.ds(row, count))]
        return send(src, dst, send_sem.at[i], recv_sem.at[i], ctx_of(shifted(co, *s.link)), tp)

    def run_close(s):
        which, half, row0, rows, order, _ = SCATTER_PLAN[s.chunk]
        dim = order[2 - s.stage]
        kept = sorted(order[: 2 - s.stage])
        own = own_at(s, block_at(half, dim, co[dim]))
        arrived = came[3 * s.chunk + s.stage]

        def total(at):
            value = own(at, 0, rows)
            for k in s.outer:
                value = value + arrived[(k, *at)].astype(F32)
            if s.stage < 2:
                sums[2 * s.chunk + s.stage][at] = value
            else:
                (dkp_ref if which == 0 else dvp_ref)[half, pl.ds(row0, rows)] = value

        blocks(kept, total)

    def run_piece(i, s):
        which, half, row0, rows, order, _ = SCATTER_PLAN[s.chunk]
        _, axis, dim = order
        where = [pl.ds(0, SIZES[d]) for d in range(3)]
        where[dim] = block_at(half, dim, shifted(co, dim, 1)[dim])
        where[axis] = block_at(half, axis, shifted(co, axis, s.offset)[axis])
        return send(
            part_hbm.at[(which, half, *where, pl.ds(row0, rows))], came[3 * s.chunk].at[s.piece],
            send_sem.at[i], recv_sem.at[i], ctx_of(shifted(co, *s.link)), tp,
        )

    def run_close_piece(s):
        which, half, row0, rows, order, _ = SCATTER_PLAN[s.chunk]
        first, axis, dim = order
        mine = block_at(half, dim, co[dim])
        target = block_at(half, axis, shifted(co, axis, s.offset)[axis])
        load(2 * which + half)

        def total(at):
            where = {first: at[0], axis: target, dim: mine}
            value = part_ref[(which, half, *(where[d] for d in range(3)), pl.ds(row0, rows))].astype(F32)
            value = value + came[3 * s.chunk][(s.piece, *at)].astype(F32)
            sums[2 * s.chunk][tuple(where[d] for d in sorted((first, axis)))] = value

        blocks([first], total)

    tap_copies = []

    def tap_start():
        k = len(tap_copies)
        tap_copies.append(send(tap_out.at[k], tap_in.at[k], tap_send.at[k], tap_recv.at[k], *partners[k]))

    def tap_sum():
        k = len(tap_copies) - 1
        tap_copies[k].wait_recv()
        return tap_out[k] + tap_in[k]

    def query_gradient():
        load(4)
        for copy in rims:
            copy.wait_recv()
        starts = doc_starts(lengths_ref)
        for half in range(2):
            p0 = c * ROWS if half == 0 else (2 * CTX - 1 - c) * ROWS
            places = p0 + lax.broadcasted_iota(jnp.int32, (ROWS, WIDTH), 0)
            ahead = [
                jnp.logical_and(places >= start_of(places + s, starts), places + s < LENGTH) for s in range(1, 3)
            ]
            for h in range(HEADS):
                lanes = slice(h * WIDTH, (h + 1) * WIDTH)
                beyond = rim_ref[half, :, lanes]
                if half == 0:
                    beyond = jnp.where(c == CTX - 1, dq_ref[1, 0:8, lanes], beyond)
                here = dq_ref[half, :, lanes]
                cat = jnp.concatenate([here, beyond], axis=0)
                y = filters_ref[0, 0:1] * here
                for s in range(1, 3):
                    y = y + jnp.where(ahead[s - 1], filters_ref[0, s : s + 1] * cat[s : s + ROWS], 0.0)
                dqp_ref[half, :, lanes] = y

    order, times = in_order(steps)
    copies, seen = {}, set()
    rims = []
    first = 0
    while steps[order[first]].link and not steps[order[first]].after and not steps[order[first]].needs:
        first += 1
    pace = (times[-1] - times[first]) / 8
    marks = {max(n for n, t in enumerate(times) if t <= times[first] + pace * k): k for k in range(1, 8)}
    for n, i in enumerate(order):
        s = steps[i]
        for j in s.after:
            if steps[j].link and j not in seen:
                copies[j].wait_recv()
                seen.add(j)
        if s.kind == "send":
            copies[i] = run_send(i, s)
        elif s.kind == "piece":
            copies[i] = run_piece(i, s)
        elif s.kind == "close":
            run_close(s)
        else:
            run_close_piece(s)
        if n + 1 == first:
            for half, target in ((0, before), (1, after)):
                rims.append(
                    send(
                        dq_hbm.at[half, pl.ds(0, 8)], rim_ref.at[half],
                        rim_send.at[half], rim_recv.at[half], target, tp,
                    )
                )
            load(5)
            tap_start()
            query_gradient()
        if n in marks:
            tap_out[marks[n]] = tap_sum()
            tap_start()
    value = tap_sum()
    for m in range(3):
        dfil_ref[m] = value[3 * m : 3 * m + 3]
    for copy in list(copies.values()) + tap_copies + rims:
        copy.wait_send()


def scatter(lengths, filters, part, dq, taps):
    vmem = pl.BlockSpec(memory_space=pltpu.VMEM)
    hbm = pl.BlockSpec(memory_space=pltpu.HBM)
    count = len(scatter_steps(SCATTER_PLAN))
    came, stash, sums = [], [], []
    for _, _, _, rows, order, ways in SCATTER_PLAN:
        for stage in range(3):
            kept = tuple(SIZES[d] for d in sorted(order[: 2 - stage]))
            if stage == 0 and order[2] == Y:
                shape = (SIZES[order[1]], SIZES[order[0]])
                spare = (1, 1)
            else:
                shape = spare = (len(WAYS[ways[2 - stage]]),) + kept
            came.append(pltpu.VMEM(shape + (rows, WIDTH), BF16))
            stash.append(pltpu.VMEM(spare + (rows, WIDTH), BF16))
            if stage < 2:
                sums.append(pltpu.VMEM(kept + (rows, WIDTH), F32))
    return pl.pallas_call(
        scatter_kernel,
        out_shape=(
            jax.ShapeDtypeStruct((2, ROWS, HEADS * WIDTH), F32),
            jax.ShapeDtypeStruct((2, ROWS, WIDTH), F32),
            jax.ShapeDtypeStruct((2, ROWS, WIDTH), F32),
            jax.ShapeDtypeStruct((3, 3, WIDTH), F32),
        ),
        in_specs=[pl.BlockSpec(memory_space=pltpu.SMEM), vmem] + [hbm] * 3,
        out_specs=(vmem,) * 4,
        scratch_shapes=came
        + stash
        + sums
        + [
            pltpu.VMEM((2, 2) + SIZES + (ROWS, WIDTH), BF16),
            pltpu.VMEM((2, ROWS, HEADS * WIDTH), F32),
            pltpu.VMEM((2, 8, HEADS * WIDTH), F32),
            pltpu.VMEM((8, 16, WIDTH), F32),
            pltpu.VMEM((8, 16, WIDTH), F32),
            pltpu.SemaphoreType.DMA((count,)),
            pltpu.SemaphoreType.DMA((count,)),
            pltpu.SemaphoreType.DMA((2,)),
            pltpu.SemaphoreType.DMA((2,)),
            pltpu.SemaphoreType.DMA((8,)),
            pltpu.SemaphoreType.DMA((8,)),
            pltpu.SemaphoreType.DMA((6,)),
        ],
        compiler_params=pltpu.CompilerParams(
            collective_id=2, has_side_effects=True, vmem_limit_bytes=60 << 20
        ),
        name="scatter",
    )(lengths, filters, part, dq, taps)


def deliver_kernel(*refs):
    count = len(refs) // 2
    for src, dst in zip(refs[:count], refs[count:]):
        dst[...] = src[...]


def deliver(*arrays):
    vmem = pl.BlockSpec(memory_space=pltpu.VMEM)
    return pl.pallas_call(
        deliver_kernel,
        out_shape=tuple(jax.ShapeDtypeStruct(a.shape, a.dtype) for a in arrays),
        in_specs=[vmem] * len(arrays),
        out_specs=(vmem,) * len(arrays),
        compiler_params=pltpu.CompilerParams(vmem_limit_bytes=60 << 20),
        name="deliver",
    )(*arrays)


def shards(q_pre, k_pre, value_before_filter, d_out, filters, doc_lengths):
    gathered, rim = gather(k_pre, value_before_filter, q_pre)
    dq, part, taps = attend(
        doc_lengths, filters, q_pre, rim, d_out, gathered.reshape(2, LENGTH, WIDTH)
    )
    part = part.reshape((2, 2) + SIZES + (ROWS, WIDTH))
    return deliver(*scatter(doc_lengths, filters, part, dq, taps))


def solution(mesh):
    split = P(None, "ctx", "tp")
    return jax.shard_map(
        shards,
        mesh=mesh,
        in_specs=(split, split, split, split, P(), P()),
        out_specs=(split, split, split, P()),
        check_vma=False,
    )
```

```python
import math

import jax
import jax.numpy as jnp
from jax import lax
from jax.experimental import pallas as pl
from jax.experimental.pallas import tpu as pltpu
from jax.sharding import PartitionSpec as P

MESH = pl.DeviceIdType.MESH
Y, X, Z = 0, 1, 2
SIZES = (2, 4, 8)
CTX = 64
TP = 4
ROWS = 64
LENGTH = 8192
HEADS = 8
WIDTH = 128
COLS = HEADS * ROWS
TILE = 512
N_TILES = LENGTH // TILE
MAX_TILES = (2 * (TILE - 1) + LENGTH // 2 + ROWS - 1) // TILE
SCALE = WIDTH ** (-0.5)
LOG2E = math.log2(math.e)
F32 = jnp.float32
BF16 = jnp.bfloat16

GATHER_PLAN = (
    (0, 0, 0, 32, (Y, X, Z), ("pair", "all4", "ring8")),
    (1, 1, 0, 32, (Y, X, Z), ("pair", "all4", "ring8")),
    (0, 1, 0, 32, (Y, X, Z), ("pair", "ring4", "ring8")),
    (1, 0, 0, 32, (X, Z, Y), ("all4", "three8", "pair")),
    (0, 0, 32, 32, (Z, Y, X), ("two8", "pair", "ring4")),
    (1, 1, 32, 32, (Z, Y, X), ("two8", "pair", "ring4")),
    (0, 1, 32, 32, (Z, Y, X), ("two8", "pair", "ring4")),
    (1, 0, 32, 32, (Z, X, Y), ("two8", "ring4", "pair")),
)
SCATTER_PLAN = GATHER_PLAN

WAYS = {
    "pair": ((1, 0, None, None),),
    "ring4": ((1, 0, None, None), (-1, 0, None, None), (1, -1, 0, 0), (-1, 1, 1, 1)),
    "all4": ((2, 0, None, None), (1, 0, None, None), (-1, 0, None, None)),
    "ring8": (
        (1, 0, None, None), (-1, 0, None, None), (1, -1, None, 0), (-1, 1, None, 1),
        (1, -2, None, 2), (-1, 2, None, 3), (1, -3, 0, 4), (-1, 3, 1, 5),
    ),
    "three8": (
        (2, 0, None, None), (-2, 0, None, None), (1, 0, None, None), (-1, 0, None, None),
        (1, -2, None, 0), (-1, 2, None, 1), (1, -3, 0, 4), (-1, 3, 1, 5),
    ),
    "two8": (
        (2, 0, None, None), (-2, 0, None, None), (1, 0, None, None), (-1, 0, None, None),
        (2, -2, 0, 0), (-2, 2, 1, 1), (1, -2, None, 0), (-1, 2, None, 1),
    ),
    "all8": (
        (4, 0, None, None), (3, 0, None, None), (-3, 0, None, None), (2, 0, None, None), (-2, 0, None, None),
        (1, 0, None, None), (-1, 0, None, None),
    ),
}

LINK, LATENCY, FURTHER, ISSUE, ADD = 54e3, 2.1, 0.6, 0.06, 0.0003
ROW_BYTES = WIDTH * 2
LAG = 32


def displacements(steps):
    found = {(s.link[0], far % SIZES[s.link[0]]) for s in steps if s.link for far in (s.link[1], -s.link[1])}
    return sorted(found)


def count_of(dims):
    return math.prod(SIZES[d] for d in dims)


class Step:
    def __init__(self, chunk, after=(), needs=(), link=None, blocks=0.0, adds=0.0, **what):
        self.chunk, self.after, self.needs, self.link = chunk, list(after), list(needs), link
        self.blocks, self.adds = blocks, adds
        self.__dict__.update(what)


def gather_steps(plan):
    steps = []

    def add(*args, **what):
        steps.append(Step(*args, **what))
        return len(steps) - 1

    for chunk, (_, _, _, rows, order, ways) in enumerate(plan):
        by_stage = []
        for stage, dim in enumerate(order):
            region = {d: None if s < stage else 0 for s, d in enumerate(order)}
            bundle = rows * count_of(order[:stage])
            here = []
            if stage == 2 and SIZES[dim] == 2:
                axis = order[1]
                region[axis] = 0
                here.append(
                    add(chunk, by_stage[0], link=(dim, 1), blocks=bundle / SIZES[axis], region=region, part=None)
                )
                for i in by_stage[1]:
                    there = dict(region)
                    there[axis] = steps[i].region[axis] - steps[i].link[1]
                    here.append(
                        add(chunk, [i], link=(dim, 1), blocks=steps[i].blocks, region=there, part=steps[i].part)
                    )
            else:
                for far, offset, part, first in WAYS[ways[stage]]:
                    there = dict(region)
                    there[dim] = offset
                    after = [here[first]] if first is not None else by_stage[-1] if stage else []
                    here.append(
                        add(
                            chunk, after, link=(dim, far), blocks=bundle * (1 if part is None else 0.5),
                            region=there, part=part,
                        )
                    )
            by_stage.append(here)
    return steps


def scatter_steps(plan):
    steps = []

    def add(*args, **what):
        steps.append(Step(*args, **what))
        return len(steps) - 1

    for chunk, (_, _, _, rows, order, ways) in enumerate(plan):
        ready = None
        for stage in range(3):
            dim = order[2 - stage]
            n = SIZES[dim]
            bundle = rows * count_of(order[: 2 - stage])
            if stage == 0 and n == 2:
                axis = order[1]
                m = SIZES[axis]
                ready = {}
                offsets = [m // 2] + [sign * o for o in range(m // 2 - 1, 0, -1) for sign in (1, -1)] + [0]
                for piece, offset in enumerate(offsets):
                    what = dict(stage=0, piece=piece, offset=offset)
                    i = add(chunk, link=(dim, 1), blocks=bundle / m, kind="piece", **what)
                    ready[offset % m] = add(chunk, [i], adds=bundle / m, kind="close_piece", **what)
                continue

            def own(offset):
                return [] if ready is None else [ready[offset % n if len(ready) > 1 else 0]]

            way = WAYS[ways[2 - stage]]
            made = {}
            for e in reversed(range(len(way))):
                far, offset, part, _ = way[e]
                inner = [k for k in range(len(way)) if way[k][3] == e]
                made[e] = add(
                    chunk, [made[k] for k in inner], own(offset - far), link=(dim, -far),
                    blocks=bundle * (1 if part is None else 0.5), adds=bundle if stage or inner else 0,
                    kind="send", stage=stage, entry=e, inner=inner, offset=offset - far, part=part,
                )
            outer = [k for k in range(len(way)) if way[k][3] is None]
            ready = {
                0: add(
                    chunk, [made[k] for k in outer], own(0), adds=bundle * len(outer),
                    kind="close", stage=stage, outer=outer,
                )
            }
    return steps


def in_order(steps):
    left = [len(s.after) + len(s.needs) for s in steps]
    users = [[] for _ in steps]
    for i, s in enumerate(steps):
        for j in s.after + s.needs:
            users[j].append(i)

    def wire(s):
        return abs(s.link[1]) * s.blocks * ROW_BYTES / LINK

    def late(s):
        return LATENCY + FURTHER * (abs(s.link[1]) - 1)

    rest = [0.0] * len(steps)
    for i in reversed(range(len(steps))):
        s = steps[i]
        own = ISSUE + s.adds * ADD + (wire(s) + late(s) if s.link else 0.0)
        rest[i] = own + max([rest[u] for u in users[i]], default=0.0)
    ready = [(0.0, -rest[i], i) for i in range(len(steps)) if left[i] == 0]
    when = [0.0] * len(steps)
    order, times, busy, now = [], [], {}, 0.0
    while ready:
        now = max(now, min(ready)[0])
        pick = min((r for r in ready if r[0] <= now), key=lambda r: r[1:])
        ready.remove(pick)
        i = pick[2]
        s = steps[i]
        order.append(i)
        times.append(now)
        now += ISSUE + s.adds * ADD
        seen = now
        if s.link:
            link = (s.link[0], s.link[1] > 0)
            busy[link] = max(now, busy.get(link, 0.0)) + wire(s)
            seen = busy[link] + late(s)
        for u in users[i]:
            when[u] = max(when[u], seen if i in steps[u].after else now)
            left[u] -= 1
            if left[u] == 0:
                ready.append((when[u], -rest[u], u))
    return order, times
def coords():
    c = lax.axis_index("ctx")
    return [c // 32, (c // 8) % 4, c % 8]


def ctx_of(co):
    return co[0] * 32 + co[1] * 8 + co[2]


def shifted(co, dim, by):
    co = list(co)
    co[dim] = (co[dim] + by + SIZES[dim]) % SIZES[dim]
    return co


def block_at(half, dim, at):
    return at if half == 0 else SIZES[dim] - 1 - at


def gather_kernel(k_ref, v_ref, q_ref, g_ref, rim_ref, send_sem, recv_sem, rim_send, rim_recv, own_sem):
    c = lax.axis_index("ctx")
    co = coords()
    after, before = (c + 1) % CTX, (c + CTX - 1) % CTX
    steps = gather_steps(GATHER_PLAN)
    neighbours = [ctx_of(shifted(co, *to)) for to in displacements(steps)] + [after, before]
    barrier = pltpu.get_barrier_semaphore()
    for neighbour in neighbours:
        pl.semaphore_signal(barrier, inc=1, device_id={"ctx": neighbour}, device_id_type=MESH)
    own = []
    for half in range(2):
        at = [block_at(half, d, co[d]) for d in range(3)]
        for which, source in ((0, k_ref), (1, v_ref)):
            copy = pltpu.make_async_copy(
                source.at[half], g_ref.at[which, half, at[0], at[1], at[2]], own_sem.at[which, half]
            )
            copy.start()
            own.append(copy)
    pl.semaphore_wait(barrier, len(neighbours))

    order, _ = in_order(steps)
    copies, rims, seen, waiting = {}, [], set(), []
    for n, i in enumerate(order):
        s = steps[i]
        for j in s.after:
            if j not in seen:
                copies[j].wait_recv()
                seen.add(j)
        which, half, row, rows, _, _ = GATHER_PLAN[s.chunk]
        at = []
        for d in range(3):
            if s.region[d] is None:
                at.append(pl.ds(0, SIZES[d]))
            else:
                at.append(block_at(half, d, shifted(co, d, s.region[d])[d]))
        if s.part is not None:
            rows = rows // 2
            row = row + s.part * rows
        ref = g_ref.at[which, half, at[0], at[1], at[2], pl.ds(row, rows)]
        if all(offset == 0 for offset in s.region.values()):
            src = (k_ref, v_ref)[which].at[half, pl.ds(row, rows)]
        else:
            src = ref
            while own:
                own.pop().wait()
        copies[i] = pltpu.make_async_remote_copy(
            src_ref=src,
            dst_ref=ref,
            send_sem=send_sem.at[i],
            recv_sem=recv_sem.at[i],
            device_id={"ctx": ctx_of(shifted(co, *s.link))},
            device_id_type=MESH,
        )
        copies[i].start()
        waiting.append(copies[i])
        if len(waiting) > LAG:
            waiting.pop(0).wait_send()
        if n == len(order) // 4:
            for side, target in ((0, after), (1, before)):
                copy = pltpu.make_async_remote_copy(
                    src_ref=q_ref.at[side, pl.ds(ROWS - 16, 16)],
                    dst_ref=rim_ref.at[side],
                    send_sem=rim_send.at[side],
                    recv_sem=rim_recv.at[side],
                    device_id={"ctx": target},
                    device_id_type=MESH,
                )
                copy.start()
                rims.append(copy)
    for i in order:
        if i not in seen:
            copies[i].wait_recv()
    for copy in rims:
        copy.wait()
    for copy in waiting:
        copy.wait_send()


def gather(k, v, q):
    count = len(gather_steps(GATHER_PLAN))
    hbm = pl.BlockSpec(memory_space=pltpu.HBM)
    return pl.pallas_call(
        gather_kernel,
        out_shape=(
            jax.ShapeDtypeStruct((2, 2) + SIZES + (ROWS, WIDTH), BF16),
            jax.ShapeDtypeStruct((2, 16, HEADS * WIDTH), BF16),
        ),
        in_specs=[hbm] * 3,
        out_specs=(hbm,) * 2,
        scratch_shapes=[
            pltpu.SemaphoreType.DMA((count,)),
            pltpu.SemaphoreType.DMA((count,)),
            pltpu.SemaphoreType.DMA((2,)),
            pltpu.SemaphoreType.DMA((2,)),
            pltpu.SemaphoreType.DMA((2, 2)),
        ],
        compiler_params=pltpu.CompilerParams(
            collective_id=1, has_side_effects=True, vmem_limit_bytes=60 << 20
        ),
        name="gather",
    )(k, v, q)


def doc_starts(lengths_ref):
    starts = [jnp.int32(0)]
    for d in range(7):
        starts.append(starts[-1] + lengths_ref[d])
    return starts


def start_of(places, starts):
    found = jnp.zeros_like(places)
    for s in starts[1:]:
        found = jnp.where(places >= s, s, found)
    return found


def attend_kernel(
    lengths_ref, filters_ref, q_hbm, rim_hbm, do_hbm, g_hbm,
    dq_ref, out_hbm, taps_ref,
    q_ref, rim_ref, do_ref, raw_ref, kc_ref, vc_ref, s_ref, dp_ref, dk_ref, dv_ref, qs_ref, dos_ref, dqt_ref,
    zero_ref, tap_ref, in_sem, tile_sem, out_sem,
):
    c = lax.axis_index("ctx")
    starts = doc_starts(lengths_ref)
    ends = (c * ROWS, (2 * CTX - 1 - c) * ROWS)
    heads, tails = [], []
    for half in range(2):
        heads.append(start_of(ends[half], starts) // TILE)
        tails.append((ends[half] + ROWS + TILE - 1) // TILE)
    spans = ((heads[0], tails[0]), (jnp.maximum(heads[1], tails[0]), tails[1]))

    def inside(tile):
        return jnp.logical_or(
            jnp.logical_and(tile >= heads[0], tile < tails[0]),
            jnp.logical_and(tile >= heads[1], tile < tails[1]),
        )

    def row_of(tile):
        return pl.multiple_of(tile * TILE, TILE)

    def over_spans(fn):
        for lo, hi in spans:
            lax.fori_loop(lo, hi, lambda tile, _: (fn(tile), 0)[1], 0)

    loads = [
        pltpu.make_async_copy(src, dst, in_sem.at[i])
        for i, (src, dst) in enumerate(((q_hbm, q_ref), (rim_hbm, rim_ref), (do_hbm, do_ref)))
    ]
    for copy in loads:
        copy.start()

    def tile_load(which, tile):
        rows = pl.ds(row_of(tile), TILE)
        return pltpu.make_async_copy(g_hbm.at[which, rows], raw_ref.at[which, rows], tile_sem.at[which, tile])

    def tile_store(which, tile, src):
        return pltpu.make_async_copy(src, out_hbm.at[which, pl.ds(row_of(tile), TILE)], out_sem.at[which, tile])

    def start_load(tile):
        for which in range(2):
            tile_load(which, tile).start()

    over_spans(start_load)
    zero_ref[...] = jnp.zeros((TILE, WIDTH), BF16)

    def over_blank(act):
        def body(tile, _):
            @pl.when(jnp.logical_not(inside(tile)))
            def _():
                for which in range(2):
                    act(tile_store(which, tile, zero_ref))

            return 0

        lax.fori_loop(0, N_TILES, body, 0)

    over_blank(lambda copy: copy.start())
    for copy in loads:
        copy.wait()

    def q_window(half, h):
        lanes = slice(h * WIDTH, (h + 1) * WIDTH)
        before = rim_ref[half, :, lanes]
        if half == 1:
            before = jnp.where(c == CTX - 1, q_ref[0, ROWS - 16 :, lanes], before)
        cat = jnp.concatenate([before.astype(F32), q_ref[half, :, lanes].astype(F32)], axis=0)
        return [cat[16 - s : 16 - s + ROWS] for s in range(3)]

    def q_masks(half):
        places = ends[half] + lax.broadcasted_iota(jnp.int32, (ROWS, WIDTH), 0)
        begin = start_of(places, starts)
        return [places - s >= begin for s in range(1, 3)]

    for half in range(2):
        masks = q_masks(half)
        for h in range(HEADS):
            x = q_window(half, h)
            y = filters_ref[0, 0:1] * x[0]
            for s in range(1, 3):
                y = y + jnp.where(masks[s - 1], filters_ref[0, s : s + 1] * x[s], 0.0)
            qs_ref[half, h * ROWS : (h + 1) * ROWS] = y.astype(BF16)
            dos_ref[half, h * ROWS : (h + 1) * ROWS] = do_ref[half, :, h * WIDTH : (h + 1) * WIDTH]

    def raw_window(which, tile):
        r0 = row_of(tile)
        before = raw_ref[which, pl.ds(pl.multiple_of(jnp.maximum(r0 - 16, 0), 16), 16)].astype(F32)
        first = jnp.logical_or(tile == heads[0], jnp.logical_and(tile == heads[1], heads[1] >= tails[0]))
        before = jnp.where(first, 0.0, before)
        cat = jnp.concatenate([before, raw_ref[which, pl.ds(r0, TILE)].astype(F32)], axis=0)
        return [cat[16 - s : 16 - s + TILE] for s in range(3)]

    def has_edge(tile):
        r0 = row_of(tile)
        found = jnp.logical_or(tile == 0, tile == N_TILES - 1)
        for s in starts[1:]:
            found = jnp.logical_or(found, jnp.logical_and(s >= r0 - 1, s <= r0 + TILE + 1))
        return found

    def both_ways(tile, fn):
        edge = has_edge(tile)

        @pl.when(edge)
        def _():
            places = row_of(tile) + lax.broadcasted_iota(jnp.int32, (TILE, WIDTH), 0)
            fn(tile, places)

        @pl.when(jnp.logical_not(edge))
        def _():
            fn(tile, None)

    def masked(mask, value):
        return value if mask is None else jnp.where(mask, value, 0.0)

    def back_masks(places):
        if places is None:
            return [None, None, None]
        begin = start_of(places, starts)
        return [None] + [places - s >= begin for s in range(1, 3)]

    def ahead_masks(places):
        if places is None:
            return [None, None, None]
        return [None] + [
            jnp.logical_and(places >= start_of(places + s, starts), places + s < LENGTH) for s in range(1, 3)
        ]

    def convolve(tile, places):
        masks = back_masks(places)
        r0 = row_of(tile)
        for which, dst in ((0, kc_ref), (1, vc_ref)):
            x = raw_window(which, tile)
            y = filters_ref[1 + which, 0:1] * x[0]
            for s in range(1, 3):
                y = y + masked(masks[s], filters_ref[1 + which, s : s + 1] * x[s])
            dst[pl.ds(r0, TILE)] = y.astype(BF16)

    def prepare(tile):
        for which in range(2):
            tile_load(which, tile).wait()
        both_ways(tile, convolve)
        r0 = row_of(tile)
        dk_ref[pl.ds(r0, TILE)] = jnp.zeros((TILE, WIDTH), F32)
        dv_ref[pl.ds(r0, TILE)] = jnp.zeros((TILE, WIDTH), F32)

    over_spans(prepare)

    NT = (((1,), (1,)), ((), ()))
    TN = (((0,), (0,)), ((), ()))
    for half in range(2):
        p0 = ends[half]
        t0, t1 = heads[half], tails[half]
        places = p0 + lax.broadcasted_iota(jnp.int32, (1, COLS), 1) % ROWS
        begin = start_of(places, starts)
        last_begin = start_of(p0 + ROWS - 1, starts)

        def stats_step(tile, carry, edge):
            m, l, w = carry
            r0 = row_of(tile)
            at = row_of(tile - t0)
            s = (
                lax.dot_general(kc_ref[pl.ds(r0, TILE)], qs_ref[half], NT, preferred_element_type=F32)
                * (SCALE * LOG2E)
            )
            if edge:
                keys = r0 + lax.broadcasted_iota(jnp.int32, (TILE, COLS), 0)
                s = jnp.where(jnp.logical_and(keys <= places, keys >= begin), s, -1e30)
            s_ref[pl.ds(at, TILE)] = s
            dp = (
                lax.dot_general(vc_ref[pl.ds(r0, TILE)], dos_ref[half], NT, preferred_element_type=F32)
                * SCALE
            )
            dp_ref[pl.ds(at, TILE)] = dp
            s = s.reshape(TILE // 8, 8, COLS)
            dp = dp.reshape(TILE // 8, 8, COLS)
            m_new = jnp.maximum(m, jnp.max(s, axis=0))
            factor = jnp.exp2(m - m_new)
            p = jnp.exp2(s - m_new[None])
            l = l * factor + jnp.sum(p, axis=0)
            w = w * factor + jnp.sum(p * dp, axis=0)
            return m_new, l, w

        carry = (jnp.full((8, COLS), -1e30, F32), jnp.zeros((8, COLS), F32), jnp.zeros((8, COLS), F32))
        e0 = jnp.minimum((last_begin + TILE - 1) // TILE, t1)
        e1 = jnp.maximum(e0, (p0 + 1) // TILE)
        for lo, hi, edge in ((t0, e0, True), (e0, e1, False), (e1, t1, True)):
            carry = lax.fori_loop(lo, hi, lambda tile, carry, edge=edge: stats_step(tile, carry, edge), carry)
        m, l, w = carry
        top = jnp.max(m, axis=0, keepdims=True)
        factor = jnp.exp2(m - top)
        total = jnp.sum(l * factor, axis=0, keepdims=True)
        lse = top + jnp.log2(total)
        mean = jnp.sum(w * factor, axis=0, keepdims=True) / total
        dqt_ref[...] = jnp.zeros((WIDTH, COLS), F32)

        def grads_step(tile, _):
            r0 = row_of(tile)
            at = row_of(tile - t0)
            p = jnp.exp2(s_ref[pl.ds(at, TILE)] - lse)
            ds = (p * (dp_ref[pl.ds(at, TILE)] - mean)).astype(BF16)
            dv_ref[pl.ds(r0, TILE)] += jnp.dot(p.astype(BF16), dos_ref[half], preferred_element_type=F32)
            dk_ref[pl.ds(r0, TILE)] += jnp.dot(ds, qs_ref[half], preferred_element_type=F32)
            dqt_ref[...] += lax.dot_general(kc_ref[pl.ds(r0, TILE)], ds, TN, preferred_element_type=F32)
            return 0

        lax.fori_loop(t0, t1, grads_step, 0)
        dq = jnp.transpose(dqt_ref[...])
        masks = q_masks(half)
        sums = [jnp.zeros((8, WIDTH), F32) for _ in range(3)]
        for h in range(HEADS):
            grad = dq[h * ROWS : (h + 1) * ROWS]
            dq_ref[half, :, h * WIDTH : (h + 1) * WIDTH] = grad
            x = q_window(half, h)
            for s in range(3):
                term = grad * x[s]
                if s:
                    term = jnp.where(masks[s - 1], term, 0.0)
                sums[s] = sums[s] + jnp.sum(term.reshape(ROWS // 8, 8, WIDTH), axis=0)
        for s in range(3):
            tap_ref[s] = sums[s] if half == 0 else tap_ref[s] + sums[s]

    tap_ref[3:9] = jnp.zeros((6, 8, WIDTH), F32)

    def finish(tile, places):
        back, ahead = back_masks(places), ahead_masks(places)
        r0 = row_of(tile)
        beyond = pl.ds(pl.multiple_of(jnp.minimum(r0 + TILE, LENGTH - 8), 8), 8)
        more = inside(tile + 1)
        for which, acc, stage in ((0, dk_ref, kc_ref), (1, dv_ref, vc_ref)):
            x = raw_window(which, tile)
            here = acc[pl.ds(r0, TILE)]
            cat = jnp.concatenate([here, jnp.where(more, acc[beyond], 0.0)], axis=0)
            y = filters_ref[1 + which, 0:1] * here
            for s in range(1, 3):
                y = y + masked(ahead[s], filters_ref[1 + which, s : s + 1] * cat[s : s + TILE])
            stage[pl.ds(r0, TILE)] = y.astype(BF16)
            for s in range(3):
                term = masked(back[s], here * x[s])
                tap_ref[3 + 3 * which + s] += jnp.sum(term.reshape(TILE // 8, 8, WIDTH), axis=0)

    def staged(which, tile):
        return (kc_ref, vc_ref)[which].at[pl.ds(row_of(tile), TILE)]

    def finish_tile(tile):
        both_ways(tile, finish)
        for which in range(2):
            tile_store(which, tile, staged(which, tile)).start()

    over_spans(finish_tile)
    taps_ref[...] = jnp.zeros((16, WIDTH), F32)
    for i in range(9):
        taps_ref[i : i + 1] = jnp.sum(tap_ref[i], axis=0, keepdims=True)

    def wait_store(tile):
        for which in range(2):
            tile_store(which, tile, staged(which, tile)).wait()

    over_spans(wait_store)
    over_blank(lambda copy: copy.wait())


def attend(lengths, filters, q, rim, d_out, gathered):
    vmem = pl.BlockSpec(memory_space=pltpu.VMEM)
    hbm = pl.BlockSpec(memory_space=pltpu.HBM)
    return pl.pallas_call(
        attend_kernel,
        out_shape=(
            jax.ShapeDtypeStruct((2, ROWS, HEADS * WIDTH), F32),
            jax.ShapeDtypeStruct((2, LENGTH, WIDTH), BF16),
            jax.ShapeDtypeStruct((16, WIDTH), F32),
        ),
        in_specs=[pl.BlockSpec(memory_space=pltpu.SMEM), vmem] + [hbm] * 4,
        out_specs=(vmem, hbm, vmem),
        scratch_shapes=[
            pltpu.VMEM((2, ROWS, HEADS * WIDTH), BF16),
            pltpu.VMEM((2, 16, HEADS * WIDTH), BF16),
            pltpu.VMEM((2, ROWS, HEADS * WIDTH), BF16),
            pltpu.VMEM((2, LENGTH, WIDTH), BF16),
            pltpu.VMEM((LENGTH, WIDTH), BF16),
            pltpu.VMEM((LENGTH, WIDTH), BF16),
            pltpu.VMEM((MAX_TILES * TILE, COLS), F32),
            pltpu.VMEM((MAX_TILES * TILE, COLS), F32),
            pltpu.VMEM((LENGTH, WIDTH), F32),
            pltpu.VMEM((LENGTH, WIDTH), F32),
            pltpu.VMEM((2, COLS, WIDTH), BF16),
            pltpu.VMEM((2, COLS, WIDTH), BF16),
            pltpu.VMEM((WIDTH, COLS), F32),
            pltpu.VMEM((TILE, WIDTH), BF16),
            pltpu.VMEM((9, 8, WIDTH), F32),
            pltpu.SemaphoreType.DMA((3,)),
            pltpu.SemaphoreType.DMA((2, N_TILES)),
            pltpu.SemaphoreType.DMA((2, N_TILES)),
        ],
        compiler_params=pltpu.CompilerParams(vmem_limit_bytes=60 << 20),
        name="attend",
    )(lengths, filters, q, rim, d_out, gathered)


def scatter_kernel(
    lengths_ref, filters_ref, part_hbm, dq_hbm, taps_hbm,
    dqp_ref, dkp_ref, dvp_ref, dfil_ref,
    *scratch,
):
    n_chunks = len(SCATTER_PLAN)
    came = scratch[: 3 * n_chunks]
    stash = scratch[3 * n_chunks : 6 * n_chunks]
    sums = scratch[6 * n_chunks : 8 * n_chunks]
    (
        part_ref, dq_ref, rim_ref, tap_ref,
        send_sem, recv_sem, rim_send, rim_recv, tap_send, tap_recv, part_sem,
    ) = scratch[8 * n_chunks :]
    c = lax.axis_index("ctx")
    tp = lax.axis_index("tp")
    co = coords()
    after, before = (c + 1) % CTX, (c + CTX - 1) % CTX
    steps = scatter_steps(SCATTER_PLAN)

    groups = [[(ctx_of(shifted(co, dim, by)), tp) for by in range(1, SIZES[dim])] for dim in (Z, X, Y)]
    groups.insert(2, [(c, (tp + by) % TP) for by in range(1, TP)])
    slots = (co[Z], co[X], tp, co[Y])
    near = set(displacements(steps)) | {(dim, by) for dim in (Z, X, Y) for by in range(1, SIZES[dim])}
    greet = [(ctx_of(shifted(co, *to)), tp) for to in sorted(near)]
    greet += [(after, tp), (before, tp)] + groups[2]
    barrier = pltpu.get_barrier_semaphore()
    for ctx, core in greet:
        pl.semaphore_signal(barrier, inc=1, device_id={"ctx": ctx, "tp": core}, device_id_type=MESH)
    loads = [
        pltpu.make_async_copy(part_hbm.at[which, half], part_ref.at[which, half], part_sem.at[2 * which + half])
        for which in range(2)
        for half in range(2)
    ]
    loads.append(pltpu.make_async_copy(dq_hbm, dq_ref, part_sem.at[4]))
    loads.append(pltpu.make_async_copy(taps_hbm, tap_ref.at[0, slots[0]], part_sem.at[5]))
    for copy in loads:
        copy.start()
    pl.semaphore_wait(barrier, len(greet))

    def send(src, dst, send_at, recv_at, ctx, core):
        copy = pltpu.make_async_remote_copy(
            src_ref=src, dst_ref=dst, send_sem=send_at, recv_sem=recv_at,
            device_id={"ctx": ctx, "tp": core}, device_id_type=MESH,
        )
        copy.start()
        return copy

    loaded = set()

    def load(i):
        if i not in loaded:
            loads[i].wait()
            loaded.add(i)

    def blocks(dims, fn):
        sizes = [SIZES[d] for d in dims]

        def body(i, _):
            at = []
            for size in reversed(sizes):
                at.append(i % size)
                i = i // size
            fn(tuple(reversed(at)))
            return 0

        if sizes:
            lax.fori_loop(0, math.prod(sizes), body, 0)
        else:
            fn(())

    def own_at(s, target):
        which, half, row0, _, order, _ = SCATTER_PLAN[s.chunk]
        dim = order[2 - s.stage]
        kept = sorted(order[: 2 - s.stage])
        dims = sorted(order[: 3 - s.stage])
        if s.stage == 0:
            load(2 * which + half)

        def value(at, row, count):
            where = dict(zip(kept, at))
            where[dim] = target
            full = tuple(where[d] for d in dims)
            if s.stage == 0:
                return part_ref[(which, half, *full, pl.ds(row0 + row, count))].astype(F32)
            return sums[2 * s.chunk + s.stage - 1][(*full, pl.ds(row, count))]

        return value

    def run_send(i, s):
        which, half, row0, rows, order, ways = SCATTER_PLAN[s.chunk]
        dim = order[2 - s.stage]
        kept = sorted(order[: 2 - s.stage])
        whole = tuple(pl.ds(0, SIZES[d]) for d in kept)
        target = block_at(half, dim, shifted(co, dim, s.offset)[dim])
        arrived = came[3 * s.chunk + s.stage]
        mid = rows // 2
        row, count = (0, rows) if s.part is None else (s.part * mid, mid)
        if s.stage == 0 and not s.inner:
            where = [pl.ds(0, SIZES[d]) for d in range(3)]
            where[dim] = target
            src = part_hbm.at[(which, half, *where, pl.ds(row0 + row, count))]
        else:
            held = stash[3 * s.chunk + s.stage]
            own = own_at(s, target)
            way = WAYS[ways[2 - s.stage]]
            split = s.part is None and any(way[k][2] is not None for k in s.inner)

            def merge(at):
                for part in (0, 1) if split else (None,):
                    lo, n = (part * mid, mid) if split else (row, count)
                    value = own(at, lo, n)
                    for k in s.inner:
                        if not split or way[k][2] in (None, part):
                            value = value + arrived[(k, *at, pl.ds(lo, n))].astype(F32)
                    held[(s.entry, *at, pl.ds(lo, n))] = value.astype(BF16)

            blocks(kept, merge)
            src = held.at[(s.entry, *whole, pl.ds(row, count))]
        dst = arrived.at[(s.entry, *whole, pl.ds(row, count))]
        return send(src, dst, send_sem.at[i], recv_sem.at[i], ctx_of(shifted(co, *s.link)), tp)

    def run_close(s):
        which, half, row0, rows, order, _ = SCATTER_PLAN[s.chunk]
        dim = order[2 - s.stage]
        kept = sorted(order[: 2 - s.stage])
        own = own_at(s, block_at(half, dim, co[dim]))
        arrived = came[3 * s.chunk + s.stage]

        def total(at):
            value = own(at, 0, rows)
            for k in s.outer:
                value = value + arrived[(k, *at)].astype(F32)
            if s.stage < 2:
                sums[2 * s.chunk + s.stage][at] = value
            else:
                (dkp_ref if which == 0 else dvp_ref)[half, pl.ds(row0, rows)] = value

        blocks(kept, total)

    def run_piece(i, s):
        which, half, row0, rows, order, _ = SCATTER_PLAN[s.chunk]
        _, axis, dim = order
        where = [pl.ds(0, SIZES[d]) for d in range(3)]
        where[dim] = block_at(half, dim, shifted(co, dim, 1)[dim])
        where[axis] = block_at(half, axis, shifted(co, axis, s.offset)[axis])
        return send(
            part_hbm.at[(which, half, *where, pl.ds(row0, rows))], came[3 * s.chunk].at[s.piece],
            send_sem.at[i], recv_sem.at[i], ctx_of(shifted(co, *s.link)), tp,
        )

    def run_close_piece(s):
        which, half, row0, rows, order, _ = SCATTER_PLAN[s.chunk]
        first, axis, dim = order
        mine = block_at(half, dim, co[dim])
        target = block_at(half, axis, shifted(co, axis, s.offset)[axis])
        load(2 * which + half)

        def total(at):
            where = {first: at[0], axis: target, dim: mine}
            value = part_ref[(which, half, *(where[d] for d in range(3)), pl.ds(row0, rows))].astype(F32)
            value = value + came[3 * s.chunk][(s.piece, *at)].astype(F32)
            sums[2 * s.chunk][tuple(where[d] for d in sorted((first, axis)))] = value

        blocks([first], total)

    tap_copies = []

    def tap_start(value):
        k = len(tap_copies)
        mine = tap_ref.at[k, slots[k]]
        if value is not None:
            mine[...] = value
        first = sum(len(group) for group in groups[:k])
        tap_copies.append(
            [
                send(mine, mine, tap_send.at[first + i], tap_recv.at[first + i], *peer)
                for i, peer in enumerate(groups[k])
            ]
        )

    def tap_sum():
        k = len(tap_copies) - 1
        for copy in tap_copies[k]:
            copy.wait_recv()
        value = tap_ref[k, 0]
        for i in range(1, len(groups[k]) + 1):
            value = value + tap_ref[k, i]
        return value

    def query_gradient():
        load(4)
        for copy in rims:
            copy.wait_recv()
        starts = doc_starts(lengths_ref)
        for half in range(2):
            p0 = c * ROWS if half == 0 else (2 * CTX - 1 - c) * ROWS
            places = p0 + lax.broadcasted_iota(jnp.int32, (ROWS, WIDTH), 0)
            ahead = [
                jnp.logical_and(places >= start_of(places + s, starts), places + s < LENGTH) for s in range(1, 3)
            ]
            for h in range(HEADS):
                lanes = slice(h * WIDTH, (h + 1) * WIDTH)
                beyond = rim_ref[half, :, lanes]
                if half == 0:
                    beyond = jnp.where(c == CTX - 1, dq_ref[1, 0:8, lanes], beyond)
                here = dq_ref[half, :, lanes]
                cat = jnp.concatenate([here, beyond], axis=0)
                y = filters_ref[0, 0:1] * here
                for s in range(1, 3):
                    y = y + jnp.where(ahead[s - 1], filters_ref[0, s : s + 1] * cat[s : s + ROWS], 0.0)
                dqp_ref[half, :, lanes] = y

    order, times = in_order(steps)
    copies, seen, waiting = {}, set(), []
    rims = []
    first = 0
    while steps[order[first]].link and not steps[order[first]].after and not steps[order[first]].needs:
        first += 1
    pace = (times[-1] - times[first]) / 4
    marks = {max(n for n, t in enumerate(times) if t <= times[first] + pace * k): k for k in range(1, 4)}
    for n, i in enumerate(order):
        s = steps[i]
        if len(waiting) > LAG:
            waiting.pop(0).wait_send()
        for j in s.after:
            if steps[j].link and j not in seen:
                copies[j].wait_recv()
                seen.add(j)
        if s.kind == "send":
            copies[i] = run_send(i, s)
            waiting.append(copies[i])
        elif s.kind == "piece":
            copies[i] = run_piece(i, s)
            waiting.append(copies[i])
        elif s.kind == "close":
            run_close(s)
        else:
            run_close_piece(s)
        if n + 1 == first:
            for half, target in ((0, before), (1, after)):
                rims.append(
                    send(
                        dq_hbm.at[half, pl.ds(0, 8)], rim_ref.at[half],
                        rim_send.at[half], rim_recv.at[half], target, tp,
                    )
                )
            load(5)
            tap_start(None)
            query_gradient()
        if n in marks:
            tap_start(tap_sum())
    value = tap_sum()
    for m in range(3):
        dfil_ref[m] = value[3 * m : 3 * m + 3]
    for copy in waiting + sum(tap_copies, []) + rims:
        copy.wait_send()


def scatter(lengths, filters, part, dq, taps):
    vmem = pl.BlockSpec(memory_space=pltpu.VMEM)
    hbm = pl.BlockSpec(memory_space=pltpu.HBM)
    count = len(scatter_steps(SCATTER_PLAN))
    came, stash, sums = [], [], []
    for _, _, _, rows, order, ways in SCATTER_PLAN:
        for stage in range(3):
            kept = tuple(SIZES[d] for d in sorted(order[: 2 - stage]))
            if stage == 0 and order[2] == Y:
                shape = (SIZES[order[1]], SIZES[order[0]])
                spare = (1, 1)
            else:
                shape = spare = (len(WAYS[ways[2 - stage]]),) + kept
            came.append(pltpu.VMEM(shape + (rows, WIDTH), BF16))
            stash.append(pltpu.VMEM(spare + (rows, WIDTH), BF16))
            if stage < 2:
                sums.append(pltpu.VMEM(kept + (rows, WIDTH), F32))
    return pl.pallas_call(
        scatter_kernel,
        out_shape=(
            jax.ShapeDtypeStruct((2, ROWS, HEADS * WIDTH), F32),
            jax.ShapeDtypeStruct((2, ROWS, WIDTH), F32),
            jax.ShapeDtypeStruct((2, ROWS, WIDTH), F32),
            jax.ShapeDtypeStruct((3, 3, WIDTH), F32),
        ),
        in_specs=[pl.BlockSpec(memory_space=pltpu.SMEM), vmem] + [hbm] * 3,
        out_specs=(vmem,) * 4,
        scratch_shapes=came
        + stash
        + sums
        + [
            pltpu.VMEM((2, 2) + SIZES + (ROWS, WIDTH), BF16),
            pltpu.VMEM((2, ROWS, HEADS * WIDTH), F32),
            pltpu.VMEM((2, 8, HEADS * WIDTH), F32),
            pltpu.VMEM((4, 8, 16, WIDTH), F32),
            pltpu.SemaphoreType.DMA((count,)),
            pltpu.SemaphoreType.DMA((count,)),
            pltpu.SemaphoreType.DMA((2,)),
            pltpu.SemaphoreType.DMA((2,)),
            pltpu.SemaphoreType.DMA((14,)),
            pltpu.SemaphoreType.DMA((14,)),
            pltpu.SemaphoreType.DMA((6,)),
        ],
        compiler_params=pltpu.CompilerParams(
            collective_id=2, has_side_effects=True, vmem_limit_bytes=60 << 20
        ),
        name="scatter",
    )(lengths, filters, part, dq, taps)


def deliver_kernel(*refs):
    count = len(refs) // 2
    for src, dst in zip(refs[:count], refs[count:]):
        dst[...] = src[...]


def deliver(*arrays):
    vmem = pl.BlockSpec(memory_space=pltpu.VMEM)
    return pl.pallas_call(
        deliver_kernel,
        out_shape=tuple(jax.ShapeDtypeStruct(a.shape, a.dtype) for a in arrays),
        in_specs=[vmem] * len(arrays),
        out_specs=(vmem,) * len(arrays),
        compiler_params=pltpu.CompilerParams(vmem_limit_bytes=60 << 20),
        name="deliver",
    )(*arrays)


def shards(q_pre, k_pre, value_before_filter, d_out, filters, doc_lengths):
    gathered, rim = gather(k_pre, value_before_filter, q_pre)
    dq, part, taps = attend(
        doc_lengths, filters, q_pre, rim, d_out, gathered.reshape(2, LENGTH, WIDTH)
    )
    part = part.reshape((2, 2) + SIZES + (ROWS, WIDTH))
    return deliver(*scatter(doc_lengths, filters, part, dq, taps))


def solution(mesh):
    split = P(None, "ctx", "tp")
    return jax.shard_map(
        shards,
        mesh=mesh,
        in_specs=(split, split, split, split, P(), P()),
        out_specs=(split, split, split, P()),
        check_vma=False,
    )
```

```python
import math

import jax
import jax.numpy as jnp
from jax import lax
from jax.experimental import pallas as pl
from jax.experimental.pallas import tpu as pltpu
from jax.sharding import PartitionSpec as P

MESH = pl.DeviceIdType.MESH
Y, X, Z = 0, 1, 2
SIZES = (2, 4, 8)
CTX = 64
TP = 4
ROWS = 64
LENGTH = 8192
HEADS = 8
WIDTH = 128
COLS = HEADS * ROWS
TILE = 512
N_TILES = LENGTH // TILE
MAX_TILES = (2 * (TILE - 1) + LENGTH // 2 + ROWS - 1) // TILE
SCALE = WIDTH ** (-0.5)
LOG2E = math.log2(math.e)
F32 = jnp.float32
BF16 = jnp.bfloat16

GATHER_PLAN = (
    (0, 0, 0, 32, (Y, X, Z), ("pair", "all4", "ring8")),
    (1, 1, 0, 32, (Y, X, Z), ("pair", "all4", "ring8")),
    (0, 1, 0, 32, (Y, X, Z), ("pair", "ring4", "ring8")),
    (1, 0, 0, 32, (X, Z, Y), ("all4", "three8", "pair")),
    (0, 0, 32, 32, (Z, Y, X), ("two8", "pair", "ring4")),
    (1, 1, 32, 32, (Z, Y, X), ("two8", "pair", "ring4")),
    (0, 1, 32, 32, (Z, Y, X), ("two8", "pair", "ring4")),
    (1, 0, 32, 32, (Z, X, Y), ("two8", "ring4", "pair")),
)
SCATTER_PLAN = GATHER_PLAN

WAYS = {
    "pair": ((1, 0, None, None),),
    "ring4": ((1, 0, None, None), (-1, 0, None, None), (1, -1, 0, 0), (-1, 1, 1, 1)),
    "all4": ((2, 0, None, None), (1, 0, None, None), (-1, 0, None, None)),
    "ring8": (
        (1, 0, None, None), (-1, 0, None, None), (1, -1, None, 0), (-1, 1, None, 1),
        (1, -2, None, 2), (-1, 2, None, 3), (1, -3, 0, 4), (-1, 3, 1, 5),
    ),
    "three8": (
        (2, 0, None, None), (-2, 0, None, None), (1, 0, None, None), (-1, 0, None, None),
        (1, -2, None, 0), (-1, 2, None, 1), (1, -3, 0, 4), (-1, 3, 1, 5),
    ),
    "two8": (
        (2, 0, None, None), (-2, 0, None, None), (1, 0, None, None), (-1, 0, None, None),
        (2, -2, 0, 0), (-2, 2, 1, 1), (1, -2, None, 0), (-1, 2, None, 1),
    ),
    "all8": (
        (4, 0, None, None), (3, 0, None, None), (-3, 0, None, None), (2, 0, None, None), (-2, 0, None, None),
        (1, 0, None, None), (-1, 0, None, None),
    ),
}

LINK, LATENCY, FURTHER, ISSUE, ADD = 65e3, 2.5, 0.6, 0.1, 0.0003
ROW_BYTES = WIDTH * 2
LAG = 32


def displacements(steps):
    found = {(s.link[0], far % SIZES[s.link[0]]) for s in steps if s.link for far in (s.link[1], -s.link[1])}
    return sorted(found)


def count_of(dims):
    return math.prod(SIZES[d] for d in dims)


class Step:
    def __init__(self, chunk, after=(), needs=(), link=None, blocks=0.0, adds=0.0, **what):
        self.chunk, self.after, self.needs, self.link = chunk, list(after), list(needs), link
        self.blocks, self.adds = blocks, adds
        self.__dict__.update(what)


def gather_steps(plan):
    steps = []

    def add(*args, **what):
        steps.append(Step(*args, **what))
        return len(steps) - 1

    for chunk, (_, _, _, rows, order, ways) in enumerate(plan):
        by_stage = []
        for stage, dim in enumerate(order):
            region = {d: None if s < stage else 0 for s, d in enumerate(order)}
            bundle = rows * count_of(order[:stage])
            here = []
            if stage == 2 and SIZES[dim] == 2:
                axis = order[1]
                region[axis] = 0
                here.append(
                    add(chunk, by_stage[0], link=(dim, 1), blocks=bundle / SIZES[axis], region=region, part=None)
                )
                for i in by_stage[1]:
                    there = dict(region)
                    there[axis] = steps[i].region[axis] - steps[i].link[1]
                    here.append(
                        add(chunk, [i], link=(dim, 1), blocks=steps[i].blocks, region=there, part=steps[i].part)
                    )
            else:
                for far, offset, part, first in WAYS[ways[stage]]:
                    there = dict(region)
                    there[dim] = offset
                    after = [here[first]] if first is not None else by_stage[-1] if stage else []
                    here.append(
                        add(
                            chunk, after, link=(dim, far), blocks=bundle * (1 if part is None else 0.5),
                            region=there, part=part,
                        )
                    )
            by_stage.append(here)
    return steps


def scatter_steps(plan):
    steps = []

    def add(*args, **what):
        steps.append(Step(*args, **what))
        return len(steps) - 1

    for chunk, (_, _, _, rows, order, ways) in enumerate(plan):
        ready = None
        for stage in range(3):
            dim = order[2 - stage]
            n = SIZES[dim]
            bundle = rows * count_of(order[: 2 - stage])
            if stage == 0 and n == 2:
                axis = order[1]
                m = SIZES[axis]
                ready = {}
                offsets = [m // 2] + [sign * o for o in range(m // 2 - 1, 0, -1) for sign in (1, -1)] + [0]
                for piece, offset in enumerate(offsets):
                    what = dict(stage=0, piece=piece, offset=offset)
                    i = add(chunk, link=(dim, 1), blocks=bundle / m, kind="piece", **what)
                    ready[offset % m] = add(chunk, [i], adds=bundle / m, kind="close_piece", **what)
                continue

            def own(offset):
                return [] if ready is None else [ready[offset % n if len(ready) > 1 else 0]]

            way = WAYS[ways[2 - stage]]
            made = {}
            for e in reversed(range(len(way))):
                far, offset, part, _ = way[e]
                inner = [k for k in range(len(way)) if way[k][3] == e]
                made[e] = add(
                    chunk, [made[k] for k in inner], own(offset - far), link=(dim, -far),
                    blocks=bundle * (1 if part is None else 0.5), adds=bundle if stage or inner else 0,
                    kind="send", stage=stage, entry=e, inner=inner, offset=offset - far, part=part,
                )
            outer = [k for k in range(len(way)) if way[k][3] is None]
            ready = {
                0: add(
                    chunk, [made[k] for k in outer], own(0), adds=bundle * len(outer),
                    kind="close", stage=stage, outer=outer,
                )
            }
    return steps


def in_order(steps):
    left = [len(s.after) + len(s.needs) for s in steps]
    users = [[] for _ in steps]
    for i, s in enumerate(steps):
        for j in s.after + s.needs:
            users[j].append(i)

    def wire(s):
        return abs(s.link[1]) * s.blocks * ROW_BYTES / LINK

    def late(s):
        return LATENCY + FURTHER * (abs(s.link[1]) - 1)

    rest = [0.0] * len(steps)
    for i in reversed(range(len(steps))):
        s = steps[i]
        own = ISSUE + s.adds * ADD + (wire(s) + late(s) if s.link else 0.0)
        rest[i] = own + max([rest[u] for u in users[i]], default=0.0)
    ready = [(0.0, -rest[i], i) for i in range(len(steps)) if left[i] == 0]
    when = [0.0] * len(steps)
    order, times, busy, now = [], [], {}, 0.0
    while ready:
        now = max(now, min(ready)[0])
        pick = min((r for r in ready if r[0] <= now), key=lambda r: r[1:])
        ready.remove(pick)
        i = pick[2]
        s = steps[i]
        order.append(i)
        times.append(now)
        now += ISSUE + s.adds * ADD
        seen = now
        if s.link:
            link = (s.link[0], s.link[1] > 0)
            busy[link] = max(now, busy.get(link, 0.0)) + wire(s)
            seen = busy[link] + late(s)
        for u in users[i]:
            when[u] = max(when[u], seen if i in steps[u].after else now)
            left[u] -= 1
            if left[u] == 0:
                ready.append((when[u], -rest[u], u))
    return order, times
def coords():
    c = lax.axis_index("ctx")
    return [c // 32, (c // 8) % 4, c % 8]


def ctx_of(co):
    return co[0] * 32 + co[1] * 8 + co[2]


def shifted(co, dim, by):
    co = list(co)
    co[dim] = (co[dim] + by + SIZES[dim]) % SIZES[dim]
    return co


def block_at(half, dim, at):
    return at if half == 0 else SIZES[dim] - 1 - at


def gather_kernel(k_ref, v_ref, q_ref, g_ref, rim_ref, send_sem, recv_sem, rim_send, rim_recv, own_sem):
    c = lax.axis_index("ctx")
    co = coords()
    after, before = (c + 1) % CTX, (c + CTX - 1) % CTX
    steps = gather_steps(GATHER_PLAN)
    neighbours = [ctx_of(shifted(co, *to)) for to in displacements(steps)] + [after, before]
    barrier = pltpu.get_barrier_semaphore()
    for neighbour in neighbours:
        pl.semaphore_signal(barrier, inc=1, device_id={"ctx": neighbour}, device_id_type=MESH)
    own = []
    for half in range(2):
        at = [block_at(half, d, co[d]) for d in range(3)]
        for which, source in ((0, k_ref), (1, v_ref)):
            copy = pltpu.make_async_copy(
                source.at[half], g_ref.at[which, half, at[0], at[1], at[2]], own_sem.at[which, half]
            )
            copy.start()
            own.append(copy)
    pl.semaphore_wait(barrier, len(neighbours))

    order, _ = in_order(steps)
    copies, rims, seen, waiting = {}, [], set(), []
    for n, i in enumerate(order):
        s = steps[i]
        for j in s.after:
            if j not in seen:
                copies[j].wait_recv()
                seen.add(j)
        which, half, row, rows, _, _ = GATHER_PLAN[s.chunk]
        at = []
        for d in range(3):
            if s.region[d] is None:
                at.append(pl.ds(0, SIZES[d]))
            else:
                at.append(block_at(half, d, shifted(co, d, s.region[d])[d]))
        if s.part is not None:
            rows = rows // 2
            row = row + s.part * rows
        ref = g_ref.at[which, half, at[0], at[1], at[2], pl.ds(row, rows)]
        if all(offset == 0 for offset in s.region.values()):
            src = (k_ref, v_ref)[which].at[half, pl.ds(row, rows)]
        else:
            src = ref
            while own:
                own.pop().wait()
        copies[i] = pltpu.make_async_remote_copy(
            src_ref=src,
            dst_ref=ref,
            send_sem=send_sem.at[i],
            recv_sem=recv_sem.at[i],
            device_id={"ctx": ctx_of(shifted(co, *s.link))},
            device_id_type=MESH,
        )
        copies[i].start()
        waiting.append(copies[i])
        if len(waiting) > LAG:
            waiting.pop(0).wait_send()
        if n == len(order) // 4:
            for side, target in ((0, after), (1, before)):
                copy = pltpu.make_async_remote_copy(
                    src_ref=q_ref.at[side, pl.ds(ROWS - 16, 16)],
                    dst_ref=rim_ref.at[side],
                    send_sem=rim_send.at[side],
                    recv_sem=rim_recv.at[side],
                    device_id={"ctx": target},
                    device_id_type=MESH,
                )
                copy.start()
                rims.append(copy)
    for i in order:
        if i not in seen:
            copies[i].wait_recv()
    for copy in rims:
        copy.wait()
    for copy in waiting:
        copy.wait_send()


def gather(k, v, q):
    count = len(gather_steps(GATHER_PLAN))
    hbm = pl.BlockSpec(memory_space=pltpu.HBM)
    return pl.pallas_call(
        gather_kernel,
        out_shape=(
            jax.ShapeDtypeStruct((2, 2) + SIZES + (ROWS, WIDTH), BF16),
            jax.ShapeDtypeStruct((2, 16, HEADS * WIDTH), BF16),
        ),
        in_specs=[hbm] * 3,
        out_specs=(hbm,) * 2,
        scratch_shapes=[
            pltpu.SemaphoreType.DMA((count,)),
            pltpu.SemaphoreType.DMA((count,)),
            pltpu.SemaphoreType.DMA((2,)),
            pltpu.SemaphoreType.DMA((2,)),
            pltpu.SemaphoreType.DMA((2, 2)),
        ],
        compiler_params=pltpu.CompilerParams(
            collective_id=1, has_side_effects=True, vmem_limit_bytes=60 << 20
        ),
        name="gather",
    )(k, v, q)


def doc_starts(lengths_ref):
    starts = [jnp.int32(0)]
    for d in range(7):
        starts.append(starts[-1] + lengths_ref[d])
    return starts


def start_of(places, starts):
    found = jnp.zeros_like(places)
    for s in starts[1:]:
        found = jnp.where(places >= s, s, found)
    return found


def attend_kernel(
    lengths_ref, filters_ref, q_hbm, rim_hbm, do_hbm, g_hbm,
    dq_hbm, out_hbm, taps_ref,
    q_ref, rim_ref, do_ref, raw_ref, kc_ref, vc_ref, s_ref, dp_ref, dk_ref, dv_ref, qs_ref, dos_ref, dqt_ref,
    zero_ref, tap_ref, dq_ref, in_sem, tile_sem, out_sem, dq_sem,
):
    c = lax.axis_index("ctx")
    starts = doc_starts(lengths_ref)
    ends = (c * ROWS, (2 * CTX - 1 - c) * ROWS)
    heads, tails = [], []
    for half in range(2):
        heads.append(start_of(ends[half], starts) // TILE)
        tails.append((ends[half] + ROWS + TILE - 1) // TILE)
    spans = ((heads[0], tails[0]), (jnp.maximum(heads[1], tails[0]), tails[1]))

    def inside(tile):
        return jnp.logical_or(
            jnp.logical_and(tile >= heads[0], tile < tails[0]),
            jnp.logical_and(tile >= heads[1], tile < tails[1]),
        )

    def row_of(tile):
        return pl.multiple_of(tile * TILE, TILE)

    def over_spans(fn):
        for lo, hi in spans:
            lax.fori_loop(lo, hi, lambda tile, _: (fn(tile), 0)[1], 0)

    loads = [
        pltpu.make_async_copy(src, dst, in_sem.at[i])
        for i, (src, dst) in enumerate(((q_hbm, q_ref), (rim_hbm, rim_ref), (do_hbm, do_ref)))
    ]
    for copy in loads:
        copy.start()

    def tile_load(which, tile):
        rows = pl.ds(row_of(tile), TILE)
        return pltpu.make_async_copy(g_hbm.at[which, rows], raw_ref.at[which, rows], tile_sem.at[which, tile])

    def tile_store(which, tile, src):
        return pltpu.make_async_copy(src, out_hbm.at[which, pl.ds(row_of(tile), TILE)], out_sem.at[which, tile])

    def start_load(tile):
        for which in range(2):
            tile_load(which, tile).start()

    over_spans(start_load)
    zero_ref[...] = jnp.zeros((TILE, WIDTH), BF16)

    def over_blank(act):
        def body(tile, _):
            @pl.when(jnp.logical_not(inside(tile)))
            def _():
                for which in range(2):
                    act(tile_store(which, tile, zero_ref))

            return 0

        lax.fori_loop(0, N_TILES, body, 0)

    over_blank(lambda copy: copy.start())
    for copy in loads:
        copy.wait()

    def q_window(half, h):
        lanes = slice(h * WIDTH, (h + 1) * WIDTH)
        before = rim_ref[half, :, lanes]
        if half == 1:
            before = jnp.where(c == CTX - 1, q_ref[0, ROWS - 16 :, lanes], before)
        cat = jnp.concatenate([before.astype(F32), q_ref[half, :, lanes].astype(F32)], axis=0)
        return [cat[16 - s : 16 - s + ROWS] for s in range(3)]

    def q_masks(half):
        places = ends[half] + lax.broadcasted_iota(jnp.int32, (ROWS, WIDTH), 0)
        begin = start_of(places, starts)
        return [places - s >= begin for s in range(1, 3)]

    for half in range(2):
        masks = q_masks(half)
        for h in range(HEADS):
            x = q_window(half, h)
            y = filters_ref[0, 0:1] * x[0]
            for s in range(1, 3):
                y = y + jnp.where(masks[s - 1], filters_ref[0, s : s + 1] * x[s], 0.0)
            qs_ref[half, h * ROWS : (h + 1) * ROWS] = y.astype(BF16)
            dos_ref[half, h * ROWS : (h + 1) * ROWS] = do_ref[half, :, h * WIDTH : (h + 1) * WIDTH]

    def raw_window(which, tile):
        r0 = row_of(tile)
        before = raw_ref[which, pl.ds(pl.multiple_of(jnp.maximum(r0 - 16, 0), 16), 16)].astype(F32)
        first = jnp.logical_or(tile == heads[0], jnp.logical_and(tile == heads[1], heads[1] >= tails[0]))
        before = jnp.where(first, 0.0, before)
        cat = jnp.concatenate([before, raw_ref[which, pl.ds(r0, TILE)].astype(F32)], axis=0)
        return [cat[16 - s : 16 - s + TILE] for s in range(3)]

    def has_edge(tile):
        r0 = row_of(tile)
        found = jnp.logical_or(tile == 0, tile == N_TILES - 1)
        for s in starts[1:]:
            found = jnp.logical_or(found, jnp.logical_and(s >= r0 - 1, s <= r0 + TILE + 1))
        return found

    def both_ways(tile, fn):
        edge = has_edge(tile)

        @pl.when(edge)
        def _():
            places = row_of(tile) + lax.broadcasted_iota(jnp.int32, (TILE, WIDTH), 0)
            fn(tile, places)

        @pl.when(jnp.logical_not(edge))
        def _():
            fn(tile, None)

    def masked(mask, value):
        return value if mask is None else jnp.where(mask, value, 0.0)

    def back_masks(places):
        if places is None:
            return [None, None, None]
        begin = start_of(places, starts)
        return [None] + [places - s >= begin for s in range(1, 3)]

    def ahead_masks(places):
        if places is None:
            return [None, None, None]
        return [None] + [
            jnp.logical_and(places >= start_of(places + s, starts), places + s < LENGTH) for s in range(1, 3)
        ]

    def convolve(tile, places):
        masks = back_masks(places)
        r0 = row_of(tile)
        for which, dst in ((0, kc_ref), (1, vc_ref)):
            x = raw_window(which, tile)
            y = filters_ref[1 + which, 0:1] * x[0]
            for s in range(1, 3):
                y = y + masked(masks[s], filters_ref[1 + which, s : s + 1] * x[s])
            dst[pl.ds(r0, TILE)] = y.astype(BF16)

    def prepare(tile):
        for which in range(2):
            tile_load(which, tile).wait()
        both_ways(tile, convolve)
        r0 = row_of(tile)
        dk_ref[pl.ds(r0, TILE)] = jnp.zeros((TILE, WIDTH), F32)
        dv_ref[pl.ds(r0, TILE)] = jnp.zeros((TILE, WIDTH), F32)

    over_spans(prepare)

    NT = (((1,), (1,)), ((), ()))
    TN = (((0,), (0,)), ((), ()))
    dq_stores = []
    for half in range(2):
        p0 = ends[half]
        t0, t1 = heads[half], tails[half]
        places = p0 + lax.broadcasted_iota(jnp.int32, (1, COLS), 1) % ROWS
        begin = start_of(places, starts)
        last_begin = start_of(p0 + ROWS - 1, starts)

        def stats_step(tile, carry, edge):
            m, l, w = carry
            r0 = row_of(tile)
            at = row_of(tile - t0)
            s = (
                lax.dot_general(kc_ref[pl.ds(r0, TILE)], qs_ref[half], NT, preferred_element_type=F32)
                * (SCALE * LOG2E)
            )
            if edge:
                keys = r0 + lax.broadcasted_iota(jnp.int32, (TILE, COLS), 0)
                s = jnp.where(jnp.logical_and(keys <= places, keys >= begin), s, -1e30)
            s_ref[pl.ds(at, TILE)] = s
            dp = (
                lax.dot_general(vc_ref[pl.ds(r0, TILE)], dos_ref[half], NT, preferred_element_type=F32)
                * SCALE
            )
            dp_ref[pl.ds(at, TILE)] = dp
            s = s.reshape(TILE // 8, 8, COLS)
            dp = dp.reshape(TILE // 8, 8, COLS)
            m_new = jnp.maximum(m, jnp.max(s, axis=0))
            factor = jnp.exp2(m - m_new)
            p = jnp.exp2(s - m_new[None])
            l = l * factor + jnp.sum(p, axis=0)
            w = w * factor + jnp.sum(p * dp, axis=0)
            return m_new, l, w

        carry = (jnp.full((8, COLS), -1e30, F32), jnp.zeros((8, COLS), F32), jnp.zeros((8, COLS), F32))
        e0 = jnp.minimum((last_begin + TILE - 1) // TILE, t1)
        e1 = jnp.maximum(e0, (p0 + 1) // TILE)
        for lo, hi, edge in ((t0, e0, True), (e0, e1, False), (e1, t1, True)):
            carry = lax.fori_loop(lo, hi, lambda tile, carry, edge=edge: stats_step(tile, carry, edge), carry)
        m, l, w = carry
        top = jnp.max(m, axis=0, keepdims=True)
        factor = jnp.exp2(m - top)
        total = jnp.sum(l * factor, axis=0, keepdims=True)
        lse = top + jnp.log2(total)
        mean = jnp.sum(w * factor, axis=0, keepdims=True) / total
        dqt_ref[...] = jnp.zeros((WIDTH, COLS), F32)

        def grads_step(tile, _):
            r0 = row_of(tile)
            at = row_of(tile - t0)
            p = jnp.exp2(s_ref[pl.ds(at, TILE)] - lse)
            ds = (p * (dp_ref[pl.ds(at, TILE)] - mean)).astype(BF16)
            dv_ref[pl.ds(r0, TILE)] += jnp.dot(p.astype(BF16), dos_ref[half], preferred_element_type=F32)
            dk_ref[pl.ds(r0, TILE)] += jnp.dot(ds, qs_ref[half], preferred_element_type=F32)
            dqt_ref[...] += lax.dot_general(kc_ref[pl.ds(r0, TILE)], ds, TN, preferred_element_type=F32)
            return 0

        lax.fori_loop(t0, t1, grads_step, 0)
        dq = jnp.transpose(dqt_ref[...])
        masks = q_masks(half)
        sums = [jnp.zeros((8, WIDTH), F32) for _ in range(3)]
        for h in range(HEADS):
            grad = dq[h * ROWS : (h + 1) * ROWS]
            dq_ref[half, :, h * WIDTH : (h + 1) * WIDTH] = grad
            x = q_window(half, h)
            for s in range(3):
                term = grad * x[s]
                if s:
                    term = jnp.where(masks[s - 1], term, 0.0)
                sums[s] = sums[s] + jnp.sum(term.reshape(ROWS // 8, 8, WIDTH), axis=0)
        for s in range(3):
            tap_ref[s] = sums[s] if half == 0 else tap_ref[s] + sums[s]
        dq_stores.append(pltpu.make_async_copy(dq_ref.at[half], dq_hbm.at[half], dq_sem.at[half]))
        dq_stores[-1].start()

    tap_ref[3:9] = jnp.zeros((6, 8, WIDTH), F32)

    def finish(tile, places):
        back, ahead = back_masks(places), ahead_masks(places)
        r0 = row_of(tile)
        beyond = pl.ds(pl.multiple_of(jnp.minimum(r0 + TILE, LENGTH - 8), 8), 8)
        more = inside(tile + 1)
        for which, acc, stage in ((0, dk_ref, kc_ref), (1, dv_ref, vc_ref)):
            x = raw_window(which, tile)
            here = acc[pl.ds(r0, TILE)]
            cat = jnp.concatenate([here, jnp.where(more, acc[beyond], 0.0)], axis=0)
            y = filters_ref[1 + which, 0:1] * here
            for s in range(1, 3):
                y = y + masked(ahead[s], filters_ref[1 + which, s : s + 1] * cat[s : s + TILE])
            stage[pl.ds(r0, TILE)] = y.astype(BF16)
            for s in range(3):
                term = masked(back[s], here * x[s])
                tap_ref[3 + 3 * which + s] += jnp.sum(term.reshape(TILE // 8, 8, WIDTH), axis=0)

    def staged(which, tile):
        return (kc_ref, vc_ref)[which].at[pl.ds(row_of(tile), TILE)]

    def finish_tile(tile):
        both_ways(tile, finish)
        for which in range(2):
            tile_store(which, tile, staged(which, tile)).start()

    over_spans(finish_tile)
    taps_ref[...] = jnp.zeros((16, WIDTH), F32)
    for i in range(9):
        taps_ref[i : i + 1] = jnp.sum(tap_ref[i], axis=0, keepdims=True)

    def wait_store(tile):
        for which in range(2):
            tile_store(which, tile, staged(which, tile)).wait()

    for copy in dq_stores:
        copy.wait()
    over_spans(wait_store)
    over_blank(lambda copy: copy.wait())


def attend(lengths, filters, q, rim, d_out, gathered):
    vmem = pl.BlockSpec(memory_space=pltpu.VMEM)
    hbm = pl.BlockSpec(memory_space=pltpu.HBM)
    return pl.pallas_call(
        attend_kernel,
        out_shape=(
            jax.ShapeDtypeStruct((2, ROWS, HEADS * WIDTH), F32),
            jax.ShapeDtypeStruct((2, LENGTH, WIDTH), BF16),
            jax.ShapeDtypeStruct((16, WIDTH), F32),
        ),
        in_specs=[pl.BlockSpec(memory_space=pltpu.SMEM), vmem] + [hbm] * 4,
        out_specs=(hbm, hbm, vmem),
        scratch_shapes=[
            pltpu.VMEM((2, ROWS, HEADS * WIDTH), BF16),
            pltpu.VMEM((2, 16, HEADS * WIDTH), BF16),
            pltpu.VMEM((2, ROWS, HEADS * WIDTH), BF16),
            pltpu.VMEM((2, LENGTH, WIDTH), BF16),
            pltpu.VMEM((LENGTH, WIDTH), BF16),
            pltpu.VMEM((LENGTH, WIDTH), BF16),
            pltpu.VMEM((MAX_TILES * TILE, COLS), F32),
            pltpu.VMEM((MAX_TILES * TILE, COLS), F32),
            pltpu.VMEM((LENGTH, WIDTH), F32),
            pltpu.VMEM((LENGTH, WIDTH), F32),
            pltpu.VMEM((2, COLS, WIDTH), BF16),
            pltpu.VMEM((2, COLS, WIDTH), BF16),
            pltpu.VMEM((WIDTH, COLS), F32),
            pltpu.VMEM((TILE, WIDTH), BF16),
            pltpu.VMEM((9, 8, WIDTH), F32),
            pltpu.VMEM((2, ROWS, HEADS * WIDTH), F32),
            pltpu.SemaphoreType.DMA((3,)),
            pltpu.SemaphoreType.DMA((2, N_TILES)),
            pltpu.SemaphoreType.DMA((2, N_TILES)),
            pltpu.SemaphoreType.DMA((2,)),
        ],
        compiler_params=pltpu.CompilerParams(vmem_limit_bytes=60 << 20),
        name="attend",
    )(lengths, filters, q, rim, d_out, gathered)


def scatter_kernel(
    lengths_ref, filters_ref, part_hbm, dq_hbm, taps_hbm,
    dqp_hbm, dkp_ref, dvp_ref, dfil_ref,
    *scratch,
):
    n_chunks = len(SCATTER_PLAN)
    came = scratch[: 3 * n_chunks]
    stash = scratch[3 * n_chunks : 6 * n_chunks]
    sums = scratch[6 * n_chunks : 8 * n_chunks]
    (
        part_ref, dq_ref, dqp_ref, rim_ref, tap_ref,
        send_sem, recv_sem, rim_send, rim_recv, tap_send, tap_recv, part_sem,
    ) = scratch[8 * n_chunks :]
    c = lax.axis_index("ctx")
    tp = lax.axis_index("tp")
    co = coords()
    after, before = (c + 1) % CTX, (c + CTX - 1) % CTX
    steps = scatter_steps(SCATTER_PLAN)

    groups = [[(ctx_of(shifted(co, dim, by)), tp) for by in range(1, SIZES[dim])] for dim in (Z, X, Y)]
    groups.insert(2, [(c, (tp + by) % TP) for by in range(1, TP)])
    slots = (co[Z], co[X], tp, co[Y])
    near = set(displacements(steps)) | {(dim, by) for dim in (Z, X, Y) for by in range(1, SIZES[dim])}
    greet = [(ctx_of(shifted(co, *to)), tp) for to in sorted(near)]
    greet += [(after, tp), (before, tp)] + groups[2]
    barrier = pltpu.get_barrier_semaphore()
    for ctx, core in greet:
        pl.semaphore_signal(barrier, inc=1, device_id={"ctx": ctx, "tp": core}, device_id_type=MESH)
    loads = [
        pltpu.make_async_copy(part_hbm.at[which, half], part_ref.at[which, half], part_sem.at[2 * which + half])
        for which in range(2)
        for half in range(2)
    ]
    loads.append(pltpu.make_async_copy(dq_hbm, dq_ref, part_sem.at[4]))
    loads.append(pltpu.make_async_copy(taps_hbm, tap_ref.at[0, slots[0]], part_sem.at[5]))
    for copy in loads:
        copy.start()
    pl.semaphore_wait(barrier, len(greet))

    def send(src, dst, send_at, recv_at, ctx, core):
        copy = pltpu.make_async_remote_copy(
            src_ref=src, dst_ref=dst, send_sem=send_at, recv_sem=recv_at,
            device_id={"ctx": ctx, "tp": core}, device_id_type=MESH,
        )
        copy.start()
        return copy

    loaded = set()

    def load(i):
        if i not in loaded:
            loads[i].wait()
            loaded.add(i)

    def blocks(dims, fn):
        sizes = [SIZES[d] for d in dims]

        def body(i, _):
            at = []
            for size in reversed(sizes):
                at.append(i % size)
                i = i // size
            fn(tuple(reversed(at)))
            return 0

        if sizes:
            lax.fori_loop(0, math.prod(sizes), body, 0)
        else:
            fn(())

    def own_at(s, target):
        which, half, row0, _, order, _ = SCATTER_PLAN[s.chunk]
        dim = order[2 - s.stage]
        kept = sorted(order[: 2 - s.stage])
        dims = sorted(order[: 3 - s.stage])
        if s.stage == 0:
            load(2 * which + half)

        def value(at, row, count):
            where = dict(zip(kept, at))
            where[dim] = target
            full = tuple(where[d] for d in dims)
            if s.stage == 0:
                return part_ref[(which, half, *full, pl.ds(row0 + row, count))].astype(F32)
            return sums[2 * s.chunk + s.stage - 1][(*full, pl.ds(row, count))]

        return value

    def run_send(i, s):
        which, half, row0, rows, order, ways = SCATTER_PLAN[s.chunk]
        dim = order[2 - s.stage]
        kept = sorted(order[: 2 - s.stage])
        whole = tuple(pl.ds(0, SIZES[d]) for d in kept)
        target = block_at(half, dim, shifted(co, dim, s.offset)[dim])
        arrived = came[3 * s.chunk + s.stage]
        mid = rows // 2
        row, count = (0, rows) if s.part is None else (s.part * mid, mid)
        if s.stage == 0 and not s.inner:
            where = [pl.ds(0, SIZES[d]) for d in range(3)]
            where[dim] = target
            src = part_hbm.at[(which, half, *where, pl.ds(row0 + row, count))]
        else:
            held = stash[3 * s.chunk + s.stage]
            own = own_at(s, target)
            way = WAYS[ways[2 - s.stage]]
            split = s.part is None and any(way[k][2] is not None for k in s.inner)

            def merge(at):
                for part in (0, 1) if split else (None,):
                    lo, n = (part * mid, mid) if split else (row, count)
                    value = own(at, lo, n)
                    for k in s.inner:
                        if not split or way[k][2] in (None, part):
                            value = value + arrived[(k, *at, pl.ds(lo, n))].astype(F32)
                    held[(s.entry, *at, pl.ds(lo, n))] = value.astype(BF16)

            blocks(kept, merge)
            src = held.at[(s.entry, *whole, pl.ds(row, count))]
        dst = arrived.at[(s.entry, *whole, pl.ds(row, count))]
        return send(src, dst, send_sem.at[i], recv_sem.at[i], ctx_of(shifted(co, *s.link)), tp)

    def run_close(s):
        which, half, row0, rows, order, _ = SCATTER_PLAN[s.chunk]
        dim = order[2 - s.stage]
        kept = sorted(order[: 2 - s.stage])
        own = own_at(s, block_at(half, dim, co[dim]))
        arrived = came[3 * s.chunk + s.stage]

        def total(at):
            value = own(at, 0, rows)
            for k in s.outer:
                value = value + arrived[(k, *at)].astype(F32)
            if s.stage < 2:
                sums[2 * s.chunk + s.stage][at] = value
            else:
                (dkp_ref if which == 0 else dvp_ref)[half, pl.ds(row0, rows)] = value

        blocks(kept, total)

    def run_piece(i, s):
        which, half, row0, rows, order, _ = SCATTER_PLAN[s.chunk]
        _, axis, dim = order
        where = [pl.ds(0, SIZES[d]) for d in range(3)]
        where[dim] = block_at(half, dim, shifted(co, dim, 1)[dim])
        where[axis] = block_at(half, axis, shifted(co, axis, s.offset)[axis])
        return send(
            part_hbm.at[(which, half, *where, pl.ds(row0, rows))], came[3 * s.chunk].at[s.piece],
            send_sem.at[i], recv_sem.at[i], ctx_of(shifted(co, *s.link)), tp,
        )

    def run_close_piece(s):
        which, half, row0, rows, order, _ = SCATTER_PLAN[s.chunk]
        first, axis, dim = order
        mine = block_at(half, dim, co[dim])
        target = block_at(half, axis, shifted(co, axis, s.offset)[axis])
        load(2 * which + half)

        def total(at):
            where = {first: at[0], axis: target, dim: mine}
            value = part_ref[(which, half, *(where[d] for d in range(3)), pl.ds(row0, rows))].astype(F32)
            value = value + came[3 * s.chunk][(s.piece, *at)].astype(F32)
            sums[2 * s.chunk][tuple(where[d] for d in sorted((first, axis)))] = value

        blocks([first], total)

    tap_copies = []

    def tap_start(value):
        k = len(tap_copies)
        mine = tap_ref.at[k, slots[k]]
        if value is not None:
            mine[...] = value
        first = sum(len(group) for group in groups[:k])
        tap_copies.append(
            [
                send(mine, mine, tap_send.at[first + i], tap_recv.at[first + i], *peer)
                for i, peer in enumerate(groups[k])
            ]
        )

    def tap_sum():
        k = len(tap_copies) - 1
        for copy in tap_copies[k]:
            copy.wait_recv()
        value = tap_ref[k, 0]
        for i in range(1, len(groups[k]) + 1):
            value = value + tap_ref[k, i]
        return value

    def query_gradient():
        load(4)
        for copy in rims:
            copy.wait_recv()
        starts = doc_starts(lengths_ref)
        for half in range(2):
            p0 = c * ROWS if half == 0 else (2 * CTX - 1 - c) * ROWS
            places = p0 + lax.broadcasted_iota(jnp.int32, (ROWS, WIDTH), 0)
            ahead = [
                jnp.logical_and(places >= start_of(places + s, starts), places + s < LENGTH) for s in range(1, 3)
            ]
            for h in range(HEADS):
                lanes = slice(h * WIDTH, (h + 1) * WIDTH)
                beyond = rim_ref[half, :, lanes]
                if half == 0:
                    beyond = jnp.where(c == CTX - 1, dq_ref[1, 0:8, lanes], beyond)
                here = dq_ref[half, :, lanes]
                cat = jnp.concatenate([here, beyond], axis=0)
                y = filters_ref[0, 0:1] * here
                for s in range(1, 3):
                    y = y + jnp.where(ahead[s - 1], filters_ref[0, s : s + 1] * cat[s : s + ROWS], 0.0)
                dqp_ref[half, :, lanes] = y
        dqp_store.start()

    order, times = in_order(steps)
    copies, seen, waiting = {}, set(), []
    dqp_store = pltpu.make_async_copy(dqp_ref, dqp_hbm, part_sem.at[6])
    rims = []
    first = 0
    while steps[order[first]].link and not steps[order[first]].after and not steps[order[first]].needs:
        first += 1
    pace = (times[-1] - times[first]) / 4
    marks = {max(n for n, t in enumerate(times) if t <= times[first] + pace * k): k for k in range(1, 4)}
    for n, i in enumerate(order):
        s = steps[i]
        if len(waiting) > LAG:
            waiting.pop(0).wait_send()
        for j in s.after:
            if steps[j].link and j not in seen:
                copies[j].wait_recv()
                seen.add(j)
        if s.kind == "send":
            copies[i] = run_send(i, s)
            waiting.append(copies[i])
        elif s.kind == "piece":
            copies[i] = run_piece(i, s)
            waiting.append(copies[i])
        elif s.kind == "close":
            run_close(s)
        else:
            run_close_piece(s)
        if n + 1 == first:
            for half, target in ((0, before), (1, after)):
                rims.append(
                    send(
                        dq_hbm.at[half, pl.ds(0, 8)], rim_ref.at[half],
                        rim_send.at[half], rim_recv.at[half], target, tp,
                    )
                )
            load(5)
            tap_start(None)
            query_gradient()
        if n in marks:
            tap_start(tap_sum())
    value = tap_sum()
    for m in range(3):
        dfil_ref[m] = value[3 * m : 3 * m + 3]
    for copy in waiting + sum(tap_copies, []) + rims:
        copy.wait_send()
    dqp_store.wait()


def scatter(lengths, filters, part, dq, taps):
    vmem = pl.BlockSpec(memory_space=pltpu.VMEM)
    hbm = pl.BlockSpec(memory_space=pltpu.HBM)
    count = len(scatter_steps(SCATTER_PLAN))
    came, stash, sums = [], [], []
    for _, _, _, rows, order, ways in SCATTER_PLAN:
        for stage in range(3):
            kept = tuple(SIZES[d] for d in sorted(order[: 2 - stage]))
            if stage == 0 and order[2] == Y:
                shape = (SIZES[order[1]], SIZES[order[0]])
                spare = (1, 1)
            else:
                shape = spare = (len(WAYS[ways[2 - stage]]),) + kept
            came.append(pltpu.VMEM(shape + (rows, WIDTH), BF16))
            stash.append(pltpu.VMEM(spare + (rows, WIDTH), BF16))
            if stage < 2:
                sums.append(pltpu.VMEM(kept + (rows, WIDTH), F32))
    return pl.pallas_call(
        scatter_kernel,
        out_shape=(
            jax.ShapeDtypeStruct((2, ROWS, HEADS * WIDTH), F32),
            jax.ShapeDtypeStruct((2, ROWS, WIDTH), F32),
            jax.ShapeDtypeStruct((2, ROWS, WIDTH), F32),
            jax.ShapeDtypeStruct((3, 3, WIDTH), F32),
        ),
        in_specs=[pl.BlockSpec(memory_space=pltpu.SMEM), vmem] + [hbm] * 3,
        out_specs=(hbm, vmem, vmem, vmem),
        scratch_shapes=came
        + stash
        + sums
        + [
            pltpu.VMEM((2, 2) + SIZES + (ROWS, WIDTH), BF16),
            pltpu.VMEM((2, ROWS, HEADS * WIDTH), F32),
            pltpu.VMEM((2, ROWS, HEADS * WIDTH), F32),
            pltpu.VMEM((2, 8, HEADS * WIDTH), F32),
            pltpu.VMEM((4, 8, 16, WIDTH), F32),
            pltpu.SemaphoreType.DMA((count,)),
            pltpu.SemaphoreType.DMA((count,)),
            pltpu.SemaphoreType.DMA((2,)),
            pltpu.SemaphoreType.DMA((2,)),
            pltpu.SemaphoreType.DMA((14,)),
            pltpu.SemaphoreType.DMA((14,)),
            pltpu.SemaphoreType.DMA((7,)),
        ],
        compiler_params=pltpu.CompilerParams(
            collective_id=2, has_side_effects=True, vmem_limit_bytes=60 << 20
        ),
        name="scatter",
    )(lengths, filters, part, dq, taps)


def deliver_kernel(*refs):
    count = len(refs) // 2
    for src, dst in zip(refs[:count], refs[count:]):
        dst[...] = src[...]


def deliver(*arrays):
    vmem = pl.BlockSpec(memory_space=pltpu.VMEM)
    return pl.pallas_call(
        deliver_kernel,
        out_shape=tuple(jax.ShapeDtypeStruct(a.shape, a.dtype) for a in arrays),
        in_specs=[vmem] * len(arrays),
        out_specs=(vmem,) * len(arrays),
        compiler_params=pltpu.CompilerParams(vmem_limit_bytes=60 << 20),
        name="deliver",
    )(*arrays)


def shards(q_pre, k_pre, value_before_filter, d_out, filters, doc_lengths):
    gathered, rim = gather(k_pre, value_before_filter, q_pre)
    dq, part, taps = attend(
        doc_lengths, filters, q_pre, rim, d_out, gathered.reshape(2, LENGTH, WIDTH)
    )
    part = part.reshape((2, 2) + SIZES + (ROWS, WIDTH))
    return deliver(*scatter(doc_lengths, filters, part, dq, taps))


def solution(mesh):
    split = P(None, "ctx", "tp")
    return jax.shard_map(
        shards,
        mesh=mesh,
        in_specs=(split, split, split, split, P(), P()),
        out_specs=(split, split, split, P()),
        check_vma=False,
    )
```
